256 devices in a mesh: gx: 4 (over y), gy: 8 (over z_lo, core), gz: 8 (over x, z_hi).
Axes of the slice: x: 4, y: 4, z: 8 (z_hi: 2, z_lo: 4; z = z_hi * 4 + z_lo), core: 2. Of those that a mesh axis runs over, the one named last changes fastest.
Arguments:
- residual_start: float32 [8, 16, 16, 81, 128], P('gx', 'gy', 'gz'), may hold values from -6 to 6
- patch_inverse: bfloat16 [8, 16, 16, 540, 540], P('gx', 'gy', 'gz'), may hold values from -0.05 to 0.4
- patch_order: int32 [8, 16, 16, 540], P('gx', 'gy', 'gz'), may hold values from 0 to 539, each once within a row
- element_matrix: float32 [8, 16, 16, 108, 108], P('gx', 'gy', 'gz'), may hold values from -1.6 to 6.5
- face_order: int32 [8, 16, 16, 6, 9], P('gx', 'gy', 'gz'), may hold values from 0 to 8, each once within a row
Outputs:
- solution: float32 [8, 16, 16, 81, 128], P('gx', 'gy', 'gz')
- residual: float32 [8, 16, 16, 81, 128], P('gx', 'gy', 'gz')
The draws below stay inside these ranges and needn't reach their ends.
Inputs may be any that keep to these rules, and one draw needn't show every extreme that they name: `patch_order`: each row lists each of the 540 canonical rows of a star once. `face_order`: each face's row lists each of its 9 degrees of freedom once.
All inputs are finite; a program needn't handle non-finite values.
Results may differ from the reference program's by a relative error of at most 0.0068.
Values may be sent and summed in bfloat16 or wider, within the bound.
A program may use at most 128 MiB of HBM per device.

```python
import math
import jax
import jax.numpy as jnp
from jax import lax

RHS = 128
INNER = 54
FACE = 9
SWEEPS = 2
OWN = 81
LOCAL = 108
PATCH = 540
EX = 8
EY = 16
EZ = 16


def draw_patch_inverse(key, part):
    first, second = jax.random.split(jax.random.fold_in(key, 11), 2)
    shape = (EX, EY, EZ, PATCH, PATCH)
    noise = jnp.clip(jax.random.normal(first, shape, jnp.float32), -4.0, 4.0) * (0.4 / math.sqrt(PATCH))
    diagonal = jax.random.uniform(second, (EX, EY, EZ, PATCH, 1), jnp.float32, 0.6, 1.4)
    eye = (jnp.arange(PATCH)[:, None] == jnp.arange(PATCH)[None, :]).astype(jnp.float32)
    matrix = noise + diagonal * eye
    return (0.125 * matrix).astype(jnp.bfloat16)


def draw_element_matrix(key, part):
    first, second, third = jax.random.split(jax.random.fold_in(key, 23), 3)
    shape = (EX, EY, EZ, LOCAL, LOCAL)
    noise = jnp.clip(jax.random.normal(first, shape, jnp.float32), -4.0, 4.0) * (0.4 / math.sqrt(LOCAL))
    diagonal = jax.random.uniform(second, (EX, EY, EZ, LOCAL, 1), jnp.float32, 0.8, 1.2)
    eye = (jnp.arange(LOCAL)[:, None] == jnp.arange(LOCAL)[None, :]).astype(jnp.float32)
    low, high = (math.log(0.5), math.log(2.0))
    coefficient = jnp.exp(jax.random.uniform(third, (EX, EY, EZ, 1, 1), jnp.float32, low, high))
    return coefficient * (noise + diagonal * eye)


def steps_of(key, dims, shards, least, high):
    loudness = 1.0
    for dim, blocks in shards:
        draws = jax.random.uniform(jax.random.fold_in(jax.random.fold_in(key, 6), dim), (blocks,), jnp.float32, least / len(shards), high / len(shards))
        loudness = loudness * jnp.repeat(jnp.exp(draws), dims[dim] // blocks).reshape((-1,) + (1,) * (len(dims) - 1 - dim))
    return loudness


def bell_draw(stream_key, extent, deviation, most, cuts=(), kind=jnp.bfloat16):
    array = jax.random.normal(stream_key, extent, jnp.float32) * deviation
    if len(cuts) > 0:
        array = steps_of(stream_key, extent, cuts, -0.22, 0.18) * array
    return jnp.clip(array, min=-most, max=most).astype(kind)


def setup_inputs(seed: int = 0) -> dict:
    splits = jax.random.split(jax.random.key(seed), 6)
    residual_start = bell_draw(splits[0], (EX, EY, EZ, OWN, RHS), 1.0, 6.0, ((0, 4), (1, 8), (2, 8)), jnp.float32)
    patch_inverse = draw_patch_inverse(jax.random.fold_in(splits[5], 71), 0)
    patch_order = jax.vmap(lambda own: jax.random.permutation(own, PATCH))(jax.random.split(splits[2], EX * EY * EZ)).reshape((EX, EY, EZ, PATCH)).astype(jnp.int32)
    element_matrix = draw_element_matrix(jax.random.fold_in(splits[5], 71), 0)
    face_order = jax.vmap(lambda own: jax.random.permutation(own, FACE))(jax.random.split(splits[4], EX * EY * EZ * 6)).reshape((EX, EY, EZ, 6, FACE)).astype(jnp.int32)
    return {"residual_start": residual_start, "patch_inverse": patch_inverse, "patch_order": patch_order, "element_matrix": element_matrix, "face_order": face_order}


def face_mask(start_y, start_z, cells_y, cells_z):
    rows = jnp.arange(INNER + 3 * FACE, dtype=jnp.int32)
    in_second = (rows >= INNER + FACE) & (rows < INNER + 2 * FACE)
    in_third = rows >= INNER + 2 * FACE
    index_y = start_y + jnp.arange(cells_y, dtype=jnp.int32)
    index_z = start_z + jnp.arange(cells_z, dtype=jnp.int32)
    removed = (in_second[None, None, :] & (index_y == 0)[:, None, None]) | (in_third[None, None, :] & (index_z == 0)[None, :, None])
    return jnp.where(removed, 0.0, 1.0).astype(jnp.float32)[None, :, :, :, None]


def star_vectors(extended, counts):
    cells_x, cells_y, cells_z = counts
    pieces = []
    for xoffset in (0, 1):
        for yoffset in (0, 1):
            for zoffset in (0, 1):
                pieces.append(extended[xoffset:xoffset + cells_x, yoffset:yoffset + cells_y, zoffset:zoffset + cells_z, :INNER])
    for first in (0, 1):
        for second in (0, 1):
            pieces.append(extended[1:1 + cells_x, first:first + cells_y, second:second + cells_z, INNER:INNER + FACE])
    for first in (0, 1):
        for second in (0, 1):
            pieces.append(extended[first:first + cells_x, 1:1 + cells_y, second:second + cells_z, INNER + FACE:INNER + 2 * FACE])
    for first in (0, 1):
        for second in (0, 1):
            pieces.append(extended[first:first + cells_x, second:second + cells_y, 1:1 + cells_z, INNER + 2 * FACE:])
    return jnp.concatenate(pieces, axis=3)


def place_corrections(solved, counts):
    total = None
    face_base = 8 * INNER
    for xoffset in (0, 1):
        for yoffset in (0, 1):
            for zoffset in (0, 1):
                member = 4 * xoffset + 2 * yoffset + zoffset
                parts = [solved[..., INNER * member:INNER * (member + 1), :]]
                blank = jnp.zeros(solved.shape[:3] + (FACE, solved.shape[4]), jnp.float32)
                start = face_base + FACE * (2 * yoffset + zoffset)
                parts.append(solved[..., start:start + FACE, :] if xoffset == 1 else blank)
                start = face_base + 4 * FACE + FACE * (2 * xoffset + zoffset)
                parts.append(solved[..., start:start + FACE, :] if yoffset == 1 else blank)
                start = face_base + 8 * FACE + FACE * (2 * xoffset + yoffset)
                parts.append(solved[..., start:start + FACE, :] if zoffset == 1 else blank)
                block = jnp.concatenate(parts, axis=3)
                block = jnp.pad(block, ((xoffset, 1 - xoffset), (yoffset, 1 - yoffset), (zoffset, 1 - zoffset), (0, 0), (0, 0)))
                total = block if total is None else total + block
    return total


def apply_patches(vectors, inverses, order):
    picked = jnp.take_along_axis(vectors, order[:, :, None], axis=1)
    solved = jnp.einsum('vts,vsr->vtr', inverses.astype(jnp.float32), picked.astype(jnp.float32))
    back = jnp.argsort(order, axis=1).astype(jnp.int32)
    return jnp.take_along_axis(solved, back[:, :, None], axis=1)


def element_change(owned, uppers, matrices, face_order):
    faces = [owned[..., INNER:INNER + FACE, :], uppers[0], owned[..., INNER + FACE:INNER + 2 * FACE, :], uppers[1], owned[..., INNER + 2 * FACE:, :], uppers[2]]
    stacked = jnp.stack(faces, axis=3)
    onehot = (face_order[..., None] == jnp.arange(FACE, dtype=jnp.int32)).astype(jnp.float32)
    high = lax.Precision.HIGHEST
    local_faces = jnp.einsum('xyzfst,xyzftr->xyzfsr', onehot, stacked, precision=high)
    shape = owned.shape
    local = jnp.concatenate([owned[..., :INNER, :], local_faces.reshape(shape[:3] + (6 * FACE, shape[4]))], axis=3)
    image = jnp.einsum('xyzij,xyzjr->xyzir', matrices, local, precision=high)
    image_faces = image[..., INNER:, :].reshape(shape[:3] + (6, FACE, shape[4]))
    out_faces = jnp.einsum('xyzfst,xyzfsr->xyzftr', onehot, image_faces, precision=high)
    own_change = jnp.concatenate([image[..., :INNER, :], out_faces[:, :, :, 0], out_faces[:, :, :, 2], out_faces[:, :, :, 4]], axis=3)
    return own_change, (out_faces[:, :, :, 1], out_faces[:, :, :, 3], out_faces[:, :, :, 5])


def reference(residual_start, patch_inverse, patch_order, element_matrix, face_order):
    mask = face_mask(0, 0, EY, EZ)
    residual = residual_start * mask
    solution = jnp.zeros_like(residual)
    columns = residual.shape[4]
    for repeat in range(SWEEPS):
        rounded = residual.astype(jnp.bfloat16)
        extended = jnp.concatenate([rounded[-1:], rounded], axis=0)
        extended = jnp.pad(extended, ((0, 0), (1, 0), (1, 0), (0, 0), (0, 0)))

        def slab(carry, index):
            window = lax.dynamic_slice_in_dim(extended, index, 2, 0)
            vectors = star_vectors(window, (1, EY, EZ)).reshape(EY * EZ, PATCH, columns)
            inverses = lax.dynamic_index_in_dim(patch_inverse, index, 0, keepdims=False).reshape(EY * EZ, PATCH, PATCH)
            order = lax.dynamic_index_in_dim(patch_order, index, 0, keepdims=False).reshape(EY * EZ, PATCH)
            solved = apply_patches(vectors, inverses, order).reshape(1, EY, EZ, PATCH, columns)
            block = place_corrections(solved, (1, EY, EZ))
            current = lax.dynamic_slice_in_dim(carry, index, 2, 0)
            return lax.dynamic_update_slice_in_dim(carry, current + block, index, 0), None

        start = jnp.zeros((EX + 1, EY + 1, EZ + 1, OWN, columns), jnp.float32)
        total, unused = lax.scan(slab, start, jnp.arange(EX, dtype=jnp.int32))
        inside = total[:, 1:, 1:]
        owned = inside[1:]
        owned = jnp.concatenate([owned[:-1], owned[-1:] + inside[:1]], axis=0) * mask
        solution = solution + owned
        blank_y = jnp.zeros_like(owned[:, :1, :, :FACE])
        blank_z = jnp.zeros_like(owned[:, :, :1, :FACE])
        upper_x = jnp.roll(owned[..., INNER:INNER + FACE, :], -1, axis=0)
        upper_y = jnp.concatenate([owned[:, 1:, :, INNER + FACE:INNER + 2 * FACE], blank_y], axis=1)
        upper_z = jnp.concatenate([owned[:, :, 1:, INNER + 2 * FACE:], blank_z], axis=2)
        own_change, terms = element_change(owned, (upper_x, upper_y, upper_z), element_matrix, face_order)
        moved_x = jnp.roll(terms[0], 1, axis=0)
        moved_y = jnp.concatenate([blank_y, terms[1][:, :-1]], axis=1)
        moved_z = jnp.concatenate([blank_z, terms[2][:, :, :-1]], axis=2)
        extra = jnp.concatenate([jnp.zeros_like(owned[..., :INNER, :]), moved_x, moved_y, moved_z], axis=3)
        residual = residual - (own_change + extra) * mask
    return solution, residual
```

```python
import jax
import jax.numpy as jnp
from jax import lax
from jax.experimental import pallas as pl
from jax.experimental.pallas import tpu as pltpu
from jax.sharding import PartitionSpec as P

INNER = 54
FACE = 9
SWEEPS = 2
PATCH = 540
LOCAL = 108
STAR = 640
WIDE = 144
BLOCK = 96
MESH = pl.DeviceIdType.MESH
F32 = jnp.float32
BF16 = jnp.bfloat16

Z_HALO = 0
EARLY_X, EARLY_Y, EARLY_XY = 1, 2, 3
LATE_X, LATE_Y, LATE_XY = 4, 5, 6
BACK_X, BACK_Y, BACK_XY = 7, 8, 9
BACK2_X, BACK2_Y, BACK2_XY = 10, 11, 12
BACK_Z = 13
IMAGE_X, IMAGE_Y = 14, 16
IMAGE_Z = 18
COPIES = 19


def star_rows(order):
    one = lambda flag: flag.astype(jnp.int32)
    place = order
    for m in range(1, 8):
        place = place + 10 * one(order >= INNER * m)
    base = 8 * INNER
    place_x = order - 122
    place_y = order + 44
    place_z = order + 72
    for f in range(1, 4):
        place_x = place_x + 55 * one(order >= base + FACE * f)
        place_y = place_y + 7 * one(order >= base + FACE * (4 + f))
        place_z = place_z + 7 * one(order >= base + FACE * (8 + f))
    place = jnp.where(order >= base, place_x, place)
    place = jnp.where(order >= base + 4 * FACE, place_y, place)
    return jnp.where(order >= base + 8 * FACE, place_z, place)


def kernel(
    start_ref, inverse_ref, order_ref, matrix_ref, faces_ref,
    solution_ref, residual_ref,
    held, stars, high, low, rim, total, change, left,
    out_x, out_y, out_xy, in_x, in_y, in_xy, out_z, in_z,
    out_ix, out_iy, out_iz, in_ix, in_iy, in_iz,
    load_sem, send_sem, recv_sem,
):
    gx, gy, gz = lax.axis_index("gx"), lax.axis_index("gy"), lax.axis_index("gz")
    count_x, count_y, count_z = lax.axis_size("gx"), lax.axis_size("gy"), lax.axis_size("gz")
    up_x, down_x = lax.rem(gx + 1, count_x), lax.rem(gx + count_x - 1, count_x)
    first_y, last_y = gy == 0, gy == count_y - 1
    first_z, last_z = gz == 0, gz == count_z - 1
    not_first_y, not_last_y = gy > 0, gy < count_y - 1
    not_first_z, not_last_z = gz > 0, gz < count_z - 1

    load = pltpu.make_async_copy(inverse_ref, held, load_sem)
    load.start()

    def blank(i, carry):
        rim[i // 27, (i // 9) % 3, (i // 3) % 3, i % 3] = jnp.zeros((BLOCK, 128), BF16)
        return carry

    lax.fori_loop(0, SWEEPS * 27, blank, 0)

    barrier = pltpu.get_barrier_semaphore()

    def greet(device):
        pl.semaphore_signal(barrier, inc=1, device_id=device, device_id_type=MESH)

    greet((up_x, gy, gz))
    greet((down_x, gy, gz))

    @pl.when(not_last_y)
    def _():
        greet((gx, gy + 1, gz))
        greet((up_x, gy + 1, gz))

    @pl.when(not_first_y)
    def _():
        greet((gx, gy - 1, gz))
        greet((down_x, gy - 1, gz))

    @pl.when(not_last_z)
    def _():
        greet((gx, gy, gz + 1))

    @pl.when(not_first_z)
    def _():
        greet((gx, gy, gz - 1))

    always = None
    routes = {}

    def route(s, number, src, dst, device, sends, receives):
        copy = pltpu.make_async_remote_copy(
            src_ref=src, dst_ref=dst, send_sem=send_sem.at[s, number], recv_sem=recv_sem.at[s, number],
            device_id=device, device_id_type=MESH,
        )
        routes[s, number] = (copy, sends, receives)

    upper_y, lower_y = gy + 1, gy - 1
    for s in range(SWEEPS):
        here = rim.at[s]
        route(s, Z_HALO, here.at[1:3, 1:3, 2, 16:96], here.at[1:3, 1:3, 0, 16:96], (gx, gy, gz + 1),
              not_last_z, not_first_z)
        for x, y, xy, layers in ((EARLY_X, EARLY_Y, EARLY_XY, slice(1, 3)), (LATE_X, LATE_Y, LATE_XY, slice(0, 1))):
            route(s, x, here.at[2, 1:3, layers], here.at[0, 1:3, layers], (up_x, gy, gz), always, always)
            route(s, y, here.at[1:3, 2, layers], here.at[1:3, 0, layers], (gx, upper_y, gz), not_last_y, not_first_y)
            route(s, xy, here.at[2, 2, layers], here.at[0, 0, layers], (up_x, upper_y, gz), not_last_y, not_first_y)
        for x, y, xy, layers in ((BACK_X, BACK_Y, BACK_XY, slice(0, 1)), (BACK2_X, BACK2_Y, BACK2_XY, slice(1, 3))):
            route(s, x, out_x.at[s, layers], in_x.at[s, layers], (down_x, gy, gz), always, always)
            route(s, y, out_y.at[s, layers], in_y.at[s, layers], (gx, lower_y, gz), not_first_y, not_last_y)
            route(s, xy, out_xy.at[s, layers], in_xy.at[s, layers], (down_x, lower_y, gz), not_first_y, not_last_y)
        route(s, BACK_Z, out_z.at[s], in_z.at[s], (gx, gy, gz - 1), not_first_z, not_last_z)
        for l in (0, 1):
            route(s, IMAGE_X + l, out_ix.at[s, l], in_ix.at[s, l], (up_x, gy, gz), always, always)
            route(s, IMAGE_Y + l, out_iy.at[s, l], in_iy.at[s, l], (gx, upper_y, gz), not_last_y, not_first_y)
        route(s, IMAGE_Z, out_iz.at[s], in_iz.at[s], (gx, gy, gz + 1), not_last_z, not_first_z)

    def if_(flag, action):
        if flag is None:
            action()
        else:
            pl.when(flag)(action)

    def send(s, *numbers):
        for number in numbers:
            copy, sends, _ = routes[s, number]
            if_(sends, copy.start)

    def receive(s, number, use=None):
        copy, _, receives = routes[s, number]

        def action():
            copy.wait_recv()
            if use is not None:
                use()

        if_(receives, action)

    def clear_left():
        @pl.when(first_y)
        def _():
            left[:, 0, :, 80:96] = jnp.zeros((2, 3, 16, 128), F32)

        @pl.when(first_z)
        def _():
            left[:, :, 0, 0:16] = jnp.zeros((2, 2, 16, 128), F32)

    left[...] = jnp.zeros_like(left)
    for x in range(2):
        for y in range(2):
            for z in range(2):
                left[x, y, z + 1, 16:79] = start_ref[x, y, z, 0:63]
                left[x, y, z + 1, 80:89] = start_ref[x, y, z, 63:72]
                left[x, y, z, 0:9] = start_ref[x, y, z, 72:81]
    clear_left()

    def round_early(s):
        for x in range(2):
            for y in range(2):
                rim[s, x + 1, y + 1, 1] = left[x, y, 1].astype(BF16)
                rim[s, x + 1, y + 1, 2, 16:96] = left[x, y, 2, 16:96].astype(BF16)

    def round_late(s):
        for x in range(2):
            for y in range(2):
                rim[s, x + 1, y + 1, 0, 0:16] = left[x, y, 0, 0:16].astype(BF16)

    round_early(0)
    round_late(0)

    met = 2 + 2 * not_last_y.astype(jnp.int32) + 2 * not_first_y.astype(jnp.int32)
    met = met + not_last_z.astype(jnp.int32) + not_first_z.astype(jnp.int32)
    pl.semaphore_wait(barrier, met)

    send(0, Z_HALO, EARLY_X, EARLY_Y, EARLY_XY)

    def blank_sums(i, carry):
        s, x, y, l = i // 48, (i // 12) % 4, (i // 3) % 4, i % 3
        total[s, x, y, l] = jnp.zeros((BLOCK, 128), F32)
        change[s, x, y, l] = jnp.zeros((BLOCK, 128), F32)
        return carry

    lax.fori_loop(0, SWEEPS * 48, blank_sums, 0)

    dims_nt = (((1,), (1,)), ((), ()))

    lane = lax.broadcasted_iota(jnp.int32, (1, LOCAL), 1)
    face = sum((lane >= INNER + FACE * f).astype(jnp.int32) for f in range(1, 6))
    slot = lane - INNER - FACE * face
    spread = (lax.broadcasted_iota(jnp.int32, (FACE, LOCAL), 0) == slot).astype(F32)
    own_face = (lax.broadcasted_iota(jnp.int32, (6, LOCAL), 0) == face) & (lane >= INNER)
    base = jnp.where(lane < INNER, 16 + lane, 0)
    for f, offset in enumerate((70, 118, 80, 128, 96, 0)):
        base = base + jnp.where((lane >= INNER) & (face == f), offset, 0)
    base = base.astype(F32)
    wide_rows = lax.broadcasted_iota(jnp.int32, (WIDE, LOCAL), 0).astype(F32)

    def element(i, z):
        x, y = i // 2, i % 2
        listed = jnp.dot(faces_ref[x, y, z].astype(F32).astype(BF16), spread.astype(BF16), preferred_element_type=F32)
        place = base + jnp.sum(jnp.where(own_face, listed, 0.0), axis=0, keepdims=True)
        pick = jnp.where(wide_rows == place, 1.0, 0.0).astype(BF16)
        matrix = matrix_ref[x, y, z]
        upper = matrix.astype(BF16)
        lower = (matrix - upper.astype(F32)).astype(BF16)
        for part, ref in ((upper, high), (lower, low)):
            rows = jnp.dot(pick, part, preferred_element_type=F32).astype(BF16)
            ref[z, i] = lax.dot_general(rows, pick, dims_nt, preferred_element_type=F32).astype(BF16)

    def elements(i, carry):
        element(i, 0)
        element(i, 1)
        return carry

    lax.fori_loop(0, 4, elements, 0)

    star_iota = lax.broadcasted_iota(jnp.int32, (STAR, PATCH), 0)

    def prepare(c, first, last):
        def vertex(i, carry):
            x, y = i // 2, i % 2
            place = star_rows(order_ref[x, y, c : c + 1, :])
            pick = jnp.where(star_iota == place, 1.0, 0.0).astype(BF16)
            rows = jnp.dot(pick, held[x, y, c], preferred_element_type=F32).astype(BF16)
            stars[c, i] = lax.dot_general(rows, pick, dims_nt, preferred_element_type=F32).astype(BF16)
            return carry

        lax.fori_loop(first, last, vertex, 0)

    def solve(s, c):
        def vertex(i, carry):
            x, y = i // 2, i % 2
            pieces = []
            for p in (0, 1):
                for q in (0, 1):
                    for r in (0, 1):
                        pieces.append(rim[s, x + p, y + q, c + r, 16:80])
            for p in (0, 1):
                for r in (0, 1):
                    pieces.append(rim[s, x + p, y + 1, c + r, 80:96])
            for p in (0, 1):
                for q in (0, 1):
                    pieces.append(rim[s, x + p, y + q, c, 0:16])
            solved = jnp.dot(stars[c, i], jnp.concatenate(pieces, axis=0), preferred_element_type=F32)
            for p in (0, 1):
                for q in (0, 1):
                    for r in (0, 1):
                        m = 64 * (4 * p + 2 * q + r)
                        total[s, x + p, y + q, c + r, 16:80] += solved[m : m + 64]
            for p in (0, 1):
                for r in (0, 1):
                    m = 512 + 16 * (2 * p + r)
                    total[s, x + p, y + 1, c + r, 80:96] += solved[m : m + 16]
            for p in (0, 1):
                for q in (0, 1):
                    m = 576 + 16 * (2 * p + q)
                    total[s, x + p, y + q, c, 0:16] += solved[m : m + 16]
            return carry

        lax.fori_loop(0, 4, vertex, 0)

    def send_back(s, layers, numbers):
        for l in layers:
            for k in (1, 2):
                out_x[s, l, k - 1, 0:96] = total[s, 0, k, l].astype(BF16)
                out_x[s, l, k - 1, 96:112] = total[s, 1, k, l, 64:80].astype(BF16)
                out_y[s, l, k - 1, 0:96] = total[s, k, 0, l].astype(BF16)
                out_y[s, l, k - 1, 96:112] = total[s, k, 1, l, 80:96].astype(BF16)
            out_xy[s, l, 0:96] = total[s, 0, 0, l].astype(BF16)
            out_xy[s, l, 96:112] = total[s, 1, 0, l, 64:80].astype(BF16)
            out_xy[s, l, 112:128] = total[s, 0, 1, l, 80:96].astype(BF16)
        send(s, *numbers)

    def take_back(s, layers, numbers):
        def from_x():
            for l in layers:
                for k in (1, 2):
                    total[s, 2, k, l] += in_x[s, l, k - 1, 0:96].astype(F32)
                    total[s, 3, k, l, 64:80] += in_x[s, l, k - 1, 96:112].astype(F32)

        def from_y():
            for l in layers:
                for k in (1, 2):
                    total[s, k, 2, l] += in_y[s, l, k - 1, 0:96].astype(F32)
                    total[s, k, 3, l, 80:96] += in_y[s, l, k - 1, 96:112].astype(F32)

        def from_xy():
            for l in layers:
                total[s, 2, 2, l] += in_xy[s, l, 0:96].astype(F32)
                total[s, 3, 2, l, 64:80] += in_xy[s, l, 96:112].astype(F32)
                total[s, 2, 3, l, 80:96] += in_xy[s, l, 112:128].astype(F32)

        for number, use in zip(numbers, (from_x, from_y, from_xy)):
            receive(s, number, use)

    def send_back_z(s):
        for x in (1, 2):
            for y in (1, 2):
                m = BLOCK * (2 * x + y - 3)
                out_z[s, m : m + BLOCK] = total[s, x, y, 0].astype(BF16)
        for k in (1, 2):
            m = 384 + 16 * (k - 1)
            out_z[s, m : m + 16] = total[s, 3, k, 0, 64:80].astype(BF16)
            out_z[s, m + 32 : m + 48] = total[s, k, 3, 0, 80:96].astype(BF16)
        send(s, BACK_Z)

    def take_back_z(s):
        def use():
            for x in (1, 2):
                for y in (1, 2):
                    m = BLOCK * (2 * x + y - 3)
                    total[s, x, y, 2] += in_z[s, m : m + BLOCK].astype(F32)
            for k in (1, 2):
                m = 384 + 16 * (k - 1)
                total[s, 3, k, 2, 64:80] += in_z[s, m : m + 16].astype(F32)
                total[s, k, 3, 2, 80:96] += in_z[s, m + 32 : m + 48].astype(F32)

        receive(s, BACK_Z, use)

    def clear_total(s):
        @pl.when(first_y)
        def _():
            total[s, 1:3, 1, :, 80:96] = jnp.zeros((2, 3, 16, 128), F32)

        @pl.when(first_z)
        def _():
            total[s, 1:3, 1:3, 0, 0:16] = jnp.zeros((2, 2, 16, 128), F32)

    def images(s, l):
        def one(i, carry):
            x, y = i // 2 + 1, i % 2 + 1
            local = jnp.concatenate(
                [
                    total[s, x, y, l],
                    total[s, x, y, l - 1, 0:16],
                    total[s, x + 1, y, l, 64:80],
                    total[s, x, y + 1, l, 80:96],
                ],
                axis=0,
            )
            upper = local.astype(BF16)
            lower = (local - upper.astype(F32)).astype(BF16)
            image = jnp.dot(high[l - 1, i], upper, preferred_element_type=F32)
            image += jnp.dot(high[l - 1, i], lower, preferred_element_type=F32)
            image += jnp.dot(low[l - 1, i], upper, preferred_element_type=F32)
            change[s, x, y, l] += image[0:96]
            change[s, x, y, l - 1, 0:16] += image[96:112]
            change[s, x + 1, y, l, 64:80] += image[112:128]
            change[s, x, y + 1, l, 80:96] += image[128:144]
            return carry

        lax.fori_loop(0, 4, one, 0)

    def send_images(s, l):
        for k in (1, 2):
            m = 16 * (k - 1)
            out_ix[s, l - 1, m : m + 16] = change[s, 3, k, l, 64:80].astype(BF16)
            out_iy[s, l - 1, m : m + 16] = change[s, k, 3, l, 80:96].astype(BF16)
        send(s, IMAGE_X + l - 1, IMAGE_Y + l - 1)
        if l == 2:
            for x in (1, 2):
                for y in (1, 2):
                    m = 16 * (2 * x + y - 3)
                    out_iz[s, m : m + 16] = change[s, x, y, 2, 0:16].astype(BF16)
            send(s, IMAGE_Z)

    def take_images(s, l):
        def from_x():
            for k in (1, 2):
                m = 16 * (k - 1)
                change[s, 1, k, l, 64:80] += in_ix[s, l - 1, m : m + 16].astype(F32)

        def from_y():
            for k in (1, 2):
                m = 16 * (k - 1)
                change[s, k, 1, l, 80:96] += in_iy[s, l - 1, m : m + 16].astype(F32)

        receive(s, IMAGE_X + l - 1, from_x)
        receive(s, IMAGE_Y + l - 1, from_y)

    def take_images_z(s):
        def use():
            for x in (1, 2):
                for y in (1, 2):
                    m = 16 * (2 * x + y - 3)
                    change[s, x, y, 0, 0:16] += in_iz[s, m : m + 16].astype(F32)

        receive(s, IMAGE_Z, use)

    def update_early(s):
        for x in (1, 2):
            for y in (1, 2):
                left[x - 1, y - 1, 1] -= change[s, x, y, 1]
                left[x - 1, y - 1, 2, 16:96] -= change[s, x, y, 2, 16:96]
        clear_left()

    def update_late(s):
        for x in (1, 2):
            for y in (1, 2):
                left[x - 1, y - 1, 0, 0:16] -= change[s, x, y, 0, 0:16]
        clear_left()

    early = (EARLY_X, EARLY_Y, EARLY_XY)
    late = (LATE_X, LATE_Y, LATE_XY)
    back = (BACK_X, BACK_Y, BACK_XY)
    back2 = (BACK2_X, BACK2_Y, BACK2_XY)

    load.wait()
    prepare(0, 0, 4)
    for s in range(SWEEPS):
        if s > 0:
            for number in early:
                receive(s, number)
            solve(s, 1)
            take_images_z(s - 1)
            update_late(s - 1)
            round_late(s)
        receive(s, Z_HALO)
        send(s, *late)
        if s == 0:
            prepare(1, 0, 2)
            for number in early:
                receive(s, number)
        for number in late:
            receive(s, number)
        solve(s, 0)
        send_back(s, (0,), back)
        if s == 0:
            prepare(1, 2, 4)
        else:
            send_back(s, (1, 2), back2)
        take_back(s, (0,), back)
        send_back_z(s)
        if s == 0:
            solve(s, 1)
            send_back(s, (1, 2), back2)
        take_back(s, (1, 2), back2)
        clear_total(s)
        images(s, 1)
        send_images(s, 1)
        take_images(s, 1)
        take_back_z(s)
        clear_total(s)
        images(s, 2)
        send_images(s, 2)
        take_images(s, 2)
        update_early(s)
        if s < SWEEPS - 1:
            round_early(s + 1)
            send(s + 1, Z_HALO, *early)

    for x in range(2):
        for y in range(2):
            for z in range(2):
                block = total[0, x + 1, y + 1, z + 1] + total[1, x + 1, y + 1, z + 1]
                solution_ref[x, y, z, 0:63] = block[16:79]
                solution_ref[x, y, z, 63:72] = block[80:89]
                lower = total[0, x + 1, y + 1, z, 0:16] + total[1, x + 1, y + 1, z, 0:16]
                solution_ref[x, y, z, 72:81] = lower[0:9]
                residual_ref[x, y, z, 0:63] = left[x, y, z + 1, 16:79]
                residual_ref[x, y, z, 63:72] = left[x, y, z + 1, 80:89]
    take_images_z(SWEEPS - 1)
    update_late(SWEEPS - 1)
    for x in range(2):
        for y in range(2):
            for z in range(2):
                residual_ref[x, y, z, 72:81] = left[x, y, z, 0:9]

    for copy, sends, _ in routes.values():
        if_(sends, copy.wait_send)


def body(residual_start, patch_inverse, patch_order, element_matrix, face_order):
    shape = jax.ShapeDtypeStruct(residual_start.shape, F32)
    vmem = pl.BlockSpec(memory_space=pltpu.VMEM)
    return pl.pallas_call(
        kernel,
        out_shape=(shape, shape),
        in_specs=[vmem, pl.BlockSpec(memory_space=pl.ANY), vmem, vmem, vmem],
        out_specs=(vmem, vmem),
        scratch_shapes=[
            pltpu.VMEM((2, 2, 2, PATCH, PATCH), BF16),
            pltpu.VMEM((2, 4, STAR, STAR), BF16),
            pltpu.VMEM((2, 4, WIDE, WIDE), BF16),
            pltpu.VMEM((2, 4, WIDE, WIDE), BF16),
            pltpu.VMEM((SWEEPS, 3, 3, 3, BLOCK, 128), BF16),
            pltpu.VMEM((SWEEPS, 4, 4, 3, BLOCK, 128), F32),
            pltpu.VMEM((SWEEPS, 4, 4, 3, BLOCK, 128), F32),
            pltpu.VMEM((2, 2, 3, BLOCK, 128), F32),
            pltpu.VMEM((SWEEPS, 3, 2, 112, 128), BF16),
            pltpu.VMEM((SWEEPS, 3, 2, 112, 128), BF16),
            pltpu.VMEM((SWEEPS, 3, 128, 128), BF16),
            pltpu.VMEM((SWEEPS, 3, 2, 112, 128), BF16),
            pltpu.VMEM((SWEEPS, 3, 2, 112, 128), BF16),
            pltpu.VMEM((SWEEPS, 3, 128, 128), BF16),
            pltpu.VMEM((SWEEPS, 448, 128), BF16),
            pltpu.VMEM((SWEEPS, 448, 128), BF16),
            pltpu.VMEM((SWEEPS, 2, 32, 128), BF16),
            pltpu.VMEM((SWEEPS, 2, 32, 128), BF16),
            pltpu.VMEM((SWEEPS, 64, 128), BF16),
            pltpu.VMEM((SWEEPS, 2, 32, 128), BF16),
            pltpu.VMEM((SWEEPS, 2, 32, 128), BF16),
            pltpu.VMEM((SWEEPS, 64, 128), BF16),
            pltpu.SemaphoreType.DMA,
            pltpu.SemaphoreType.DMA((SWEEPS, COPIES)),
            pltpu.SemaphoreType.DMA((SWEEPS, COPIES)),
        ],
        compiler_params=pltpu.CompilerParams(
            collective_id=0, has_side_effects=True, vmem_limit_bytes=48 * 1024 * 1024
        ),
    )(residual_start, patch_inverse, patch_order, element_matrix, face_order)


def solution(mesh):
    return jax.shard_map(
        body,
        mesh=mesh,
        in_specs=(
            P("gx", "gy", "gz", None, None),
            P("gx", "gy", "gz", None, None),
            P("gx", "gy", "gz", None),
            P("gx", "gy", "gz", None, None),
            P("gx", "gy", "gz", None, None),
        ),
        out_specs=(P("gx", "gy", "gz", None, None), P("gx", "gy", "gz", None, None)),
        check_vma=False,
    )
```

```python
import functools

import jax
import jax.numpy as jnp
from jax import lax
from jax.experimental import pallas as pl
from jax.experimental.pallas import tpu as pltpu
from jax.sharding import PartitionSpec as P

INNER = 54
FACE = 9
SWEEPS = 2
PATCH = 540
LOCAL = 108
STAR = 640
WIDE = 144
BLOCK = 96
MESH = pl.DeviceIdType.MESH
F32 = jnp.float32
BF16 = jnp.bfloat16

Z_HALO = 0
EARLY_X, EARLY_Y, EARLY_XY = 1, 2, 3
LATE_X, LATE_Y, LATE_XY = 4, 5, 6
BACK_X, BACK_Y, BACK_XY = 7, 8, 9
BACK2_X, BACK2_Y, BACK2_XY = 10, 11, 12
BACK_Z = 13
IMAGE_X, IMAGE_Y = 14, 16
IMAGE_Z = 18
Z_UPPER, Z_LOWER, Z_FACE, Z_LAST_X, Z_LAST_Y = 19, 20, 21, 22, 23
BACK_Z_FIRST, BACK_Z_Y, BACK_Z_X = 24, 25, 26
Z_FIRST, Z_SECOND = 27, 28
COPIES = 29

CELL_ROWS = [64 * (m // 2) + 352 * (m % 2) for m in range(8)]
Y_ROWS = [256 + 16 * (g // 2) + (608 - 256) * (g % 2) for g in range(4)]
Z_ROWS = [288 + 16 * h for h in range(4)]
LOWER = 352
SEGMENTS = (
    [(INNER * m, CELL_ROWS[m]) for m in range(8)]
    + [(8 * INNER + FACE * f, CELL_ROWS[4 + f] + INNER) for f in range(4)]
    + [(8 * INNER + FACE * (4 + g), Y_ROWS[g]) for g in range(4)]
    + [(8 * INNER + FACE * (8 + h), Z_ROWS[h]) for h in range(4)]
)


def star_rows(order):
    place, shift = order, 0
    for first, row in SEGMENTS:
        step = row - first - shift
        shift += step
        if step:
            place = place + step * (order >= first).astype(jnp.int32)
    return place


def kernel(
    start_any, inverse_any, order_any, matrix_any, faces_any,
    solution_ref, residual_ref,
    start_ref, order_ref, matrix_ref, faces_ref, pairs, wide, held, stars, high, low, rim, total, change, left,
    out_x, out_y, out_xy, in_x, in_y, in_xy, out_z, in_z,
    out_ix, out_iy, out_iz, in_ix, in_iy, in_iz,
    load_sem, send_sem, recv_sem,
):
    gx, gy, gz = lax.axis_index("gx"), lax.axis_index("gy"), lax.axis_index("gz")
    count_x, count_y, count_z = lax.axis_size("gx"), lax.axis_size("gy"), lax.axis_size("gz")
    up_x, down_x = lax.rem(gx + 1, count_x), lax.rem(gx + count_x - 1, count_x)
    first_y, last_y = gy == 0, gy == count_y - 1
    first_z, last_z = gz == 0, gz == count_z - 1
    not_first_y, not_last_y = gy > 0, gy < count_y - 1
    not_first_z, not_last_z = gz > 0, gz < count_z - 1

    barrier = pltpu.get_barrier_semaphore()

    def greet(device):
        pl.semaphore_signal(barrier, inc=1, device_id=device, device_id_type=MESH)

    greet((up_x, gy, gz))
    greet((down_x, gy, gz))

    @pl.when(not_last_y)
    def _():
        greet((gx, gy + 1, gz))
        greet((up_x, gy + 1, gz))

    @pl.when(not_first_y)
    def _():
        greet((gx, gy - 1, gz))
        greet((down_x, gy - 1, gz))

    @pl.when(not_last_z)
    def _():
        greet((gx, gy, gz + 1))

    @pl.when(not_first_z)
    def _():
        greet((gx, gy, gz - 1))

    inverses = inverse_any.reshape(2, 2, 2 * PATCH, PATCH)
    loads = [pltpu.make_async_copy(start_any, start_ref, load_sem.at[0])]
    for x in range(2):
        for y in range(2):
            loads.append(pltpu.make_async_copy(inverses.at[x, y], pairs.at[x, y], load_sem.at[1 + 2 * x + y]))
    loads.append(pltpu.make_async_copy(order_any, order_ref, load_sem.at[5]))
    loads.append(pltpu.make_async_copy(matrix_any, matrix_ref, load_sem.at[6]))
    loads.append(pltpu.make_async_copy(faces_any, faces_ref, load_sem.at[7]))
    for load in loads:
        load.start()

    def blank(x, y, layers, rows):
        for s in range(SWEEPS):
            for l in layers:
                rim[s, x, y, l, rows] = jnp.zeros((rows.stop - rows.start, 128), BF16)

    for x in (1, 2):
        for y in (1, 2):
            blank(x, y, (2,), slice(0, 16))

    @pl.when(first_y)
    def _():
        for x in range(3):
            blank(x, 0, (0, 1, 2), slice(0, 96))

    @pl.when(first_z)
    def _():
        for x in (1, 2):
            for y in (1, 2):
                blank(x, y, (0,), slice(16, 96))

    always = None
    routes = {}

    def route(s, number, src, dst, device, sends, receives):
        copy = pltpu.make_async_remote_copy(
            src_ref=src, dst_ref=dst, send_sem=send_sem.at[s, number], recv_sem=recv_sem.at[s, number],
            device_id=device, device_id_type=MESH,
        )
        routes[s, number] = (copy, sends, receives)

    upper_y, lower_y = gy + 1, gy - 1
    for s in range(SWEEPS):
        here = rim.at[s]
        parts = (
            (Z_FIRST, slice(2, 3), slice(1, 3), slice(16, 96)),
            (Z_SECOND, slice(1, 2), slice(2, 3), slice(16, 96)),
            (Z_HALO, slice(1, 2), slice(1, 2), slice(16, 96)),
        )
        if s > 0:
            parts = (
                (Z_UPPER, slice(2, 3), slice(1, 3), slice(16, 80)),
                (Z_LOWER, slice(1, 2), slice(1, 3), slice(16, 64)),
                (Z_FACE, slice(1, 3), slice(2, 3), slice(80, 96)),
                (Z_LAST_X, slice(1, 2), slice(1, 3), slice(64, 80)),
                (Z_LAST_Y, slice(1, 3), slice(1, 2), slice(80, 96)),
            )
        for number, x, y, rows in parts:
            route(s, number, here.at[x, y, 2, rows], here.at[x, y, 0, rows], (gx, gy, gz + 1),
                  not_last_z, not_first_z)
        for x, y, xy, layers in ((EARLY_X, EARLY_Y, EARLY_XY, slice(1, 3)), (LATE_X, LATE_Y, LATE_XY, slice(0, 1))):
            route(s, x, here.at[2, 1:3, layers], here.at[0, 1:3, layers], (up_x, gy, gz), always, always)
            route(s, y, here.at[1:3, 2, layers], here.at[1:3, 0, layers], (gx, upper_y, gz), not_last_y, not_first_y)
            route(s, xy, here.at[2, 2, layers], here.at[0, 0, layers], (up_x, upper_y, gz), not_last_y, not_first_y)
        for x, y, xy, layers in ((BACK_X, BACK_Y, BACK_XY, slice(0, 1)), (BACK2_X, BACK2_Y, BACK2_XY, slice(1, 3))):
            route(s, x, out_x.at[s, layers], in_x.at[s, layers], (down_x, gy, gz), always, always)
            route(s, y, out_y.at[s, layers], in_y.at[s, layers], (gx, lower_y, gz), not_first_y, not_last_y)
            route(s, xy, out_xy.at[s, layers], in_xy.at[s, layers], (down_x, lower_y, gz), not_first_y, not_last_y)
        for number, rows in (
            (BACK_Z_FIRST, slice(0, 96)),
            (BACK_Z_Y, slice(96, 192)),
            (BACK_Z_X, slice(192, 288)),
            (BACK_Z, slice(288, 448)),
        ):
            route(s, number, out_z.at[s, rows], in_z.at[s, rows], (gx, gy, gz - 1), not_first_z, not_last_z)
        for l in (0, 1):
            route(s, IMAGE_X + l, out_ix.at[s, l], in_ix.at[s, l], (up_x, gy, gz), always, always)
            route(s, IMAGE_Y + l, out_iy.at[s, l], in_iy.at[s, l], (gx, upper_y, gz), not_last_y, not_first_y)
        route(s, IMAGE_Z, out_iz.at[s], in_iz.at[s], (gx, gy, gz + 1), not_last_z, not_first_z)

    def if_(flag, action):
        if flag is None:
            action()
        else:
            pl.when(flag)(action)

    def send(s, *numbers):
        for number in numbers:
            copy, sends, _ = routes[s, number]
            if_(sends, copy.start)

    def receive(s, number, use=None):
        copy, _, receives = routes[s, number]

        def action():
            copy.wait_recv()
            if use is not None:
                use()

        if_(receives, action)

    def clear_left():
        @pl.when(first_y)
        def _():
            left[:, 0, :, 80:96] = jnp.zeros((2, 3, 16, 128), F32)

        @pl.when(first_z)
        def _():
            left[:, :, 0, 0:16] = jnp.zeros((2, 2, 16, 128), F32)

    left[...] = jnp.zeros_like(left)
    loads[0].wait()
    for x in range(2):
        for y in range(2):
            for z in range(2):
                left[x, y, z + 1, 16:79] = start_ref[x, y, 0:63, z, :]
                left[x, y, z + 1, 80:89] = start_ref[x, y, 63:72, z, :]
                left[x, y, z, 0:9] = start_ref[x, y, 72:81, z, :]
    clear_left()

    def round_early(s):
        for x in range(2):
            for y in range(2):
                rim[s, x + 1, y + 1, 1] = left[x, y, 1].astype(BF16)
                rim[s, x + 1, y + 1, 2, 16:96] = left[x, y, 2, 16:96].astype(BF16)

    def round_late(s):
        for x in range(2):
            for y in range(2):
                rim[s, x + 1, y + 1, 0, 0:16] = left[x, y, 0, 0:16].astype(BF16)

    def round_faces(s):
        for l in (1, 2):
            for k in range(2):
                rim[s, 1, k + 1, l, 64:80] = left[0, k, l, 64:80].astype(BF16)
                rim[s, k + 1, 1, l, 80:96] = left[k, 0, l, 80:96].astype(BF16)

    round_early(0)
    round_late(0)

    met = 2 + 2 * not_last_y.astype(jnp.int32) + 2 * not_first_y.astype(jnp.int32)
    met = met + not_last_z.astype(jnp.int32) + not_first_z.astype(jnp.int32)
    pl.semaphore_wait(barrier, met)

    send(0, Z_FIRST, Z_SECOND, Z_HALO)

    def blank_total(s):
        def one(i, carry):
            total[s, i // 12, (i // 3) % 4, i % 3] = jnp.zeros((BLOCK, 128), F32)
            return carry

        lax.fori_loop(0, 48, one, 0)

    def blank_change():
        def one(i, carry):
            change[i // 48, (i // 12) % 4, (i // 3) % 4, i % 3] = jnp.zeros((BLOCK, 128), F32)
            return carry

        lax.fori_loop(0, SWEEPS * 48, one, 0)

    dims_nt = (((1,), (1,)), ((), ()))

    lane = lax.broadcasted_iota(jnp.int32, (1, LOCAL), 1)
    face = sum((lane >= INNER + FACE * f).astype(jnp.int32) for f in range(1, 6))
    slot = lane - INNER - FACE * face
    spread = (lax.broadcasted_iota(jnp.int32, (FACE, LOCAL), 0) == slot).astype(F32)
    own_face = (lax.broadcasted_iota(jnp.int32, (6, LOCAL), 0) == face) & (lane >= INNER)
    base = jnp.where(lane < INNER, 16 + lane, 0)
    for f, offset in enumerate((70, 118, 80, 128, 96, 0)):
        base = base + jnp.where((lane >= INNER) & (face == f), offset, 0)
    base = base.astype(F32)
    wide_rows = lax.broadcasted_iota(jnp.int32, (WIDE, LOCAL), 0).astype(F32)

    def element(i, z):
        x, y = i // 2, i % 2
        listed = jnp.dot(faces_ref[x, y, :, z, :].astype(F32).astype(BF16), spread.astype(BF16), preferred_element_type=F32)
        place = base + jnp.sum(jnp.where(own_face, listed, 0.0), axis=0, keepdims=True)
        pick = jnp.where(wide_rows == place, 1.0, 0.0).astype(BF16)
        matrix = matrix_ref[x, y, :, z, :]
        upper = matrix.astype(BF16)
        lower = (matrix - upper.astype(F32)).astype(BF16)
        for part, ref in ((upper, high), (lower, low)):
            rows = jnp.dot(pick, part, preferred_element_type=F32).astype(BF16)
            ref[z, i] = lax.dot_general(rows, pick, dims_nt, preferred_element_type=F32).astype(BF16)

    def elements(i, carry):
        element(i, 0)
        element(i, 1)
        return carry


    star_iota = lax.broadcasted_iota(jnp.int32, (STAR, PATCH), 0)

    def prepare(c, first, last):
        def vertex(i, carry):
            x, y = i // 2, i % 2
            place = star_rows(order_ref[x, y, c : c + 1, :])
            pick = jnp.where(star_iota == place, 1.0, 0.0).astype(BF16)
            rows = jnp.dot(pick, held[x, y, c], preferred_element_type=F32).astype(BF16)
            stars[c, i] = lax.dot_general(rows, pick, dims_nt, preferred_element_type=F32).astype(BF16)
            return carry

        lax.fori_loop(first, last, vertex, 0)

    def star(s, c, x, y):
        pieces = []
        for p in (0, 1):
            for q in (0, 1):
                pieces.append(rim[s, x + p, y + q, c, 16:80])
        for p in (0, 1):
            pieces.append(rim[s, x + p, y + 1, c, 80:96])
        for p in (0, 1):
            for q in (0, 1):
                pieces.append(rim[s, x + p, y + q, c, 0:16])
        for p in (0, 1):
            for q in (0, 1):
                pieces.append(rim[s, x + p, y + q, c + 1, 16:80])
        for p in (0, 1):
            pieces.append(rim[s, x + p, y + 1, c + 1, 80:96])
        return jnp.concatenate(pieces, axis=0)

    def solve(s, c, upper):
        first, last = (LOWER, STAR) if upper else (0, LOWER)
        solved = {}
        for x in (0, 1):
            for y in (0, 1):
                solved[x, y] = jnp.dot(stars[c, 2 * x + y, first:last], star(s, c, x, y), preferred_element_type=F32)
        l = c + 1 if upper else c
        for x in range(3):
            for y in range(3):
                near = [(x - p, y - q, p, q) for p in (0, 1) for q in (0, 1) if 0 <= x - p < 2 and 0 <= y - q < 2]
                cell = [solved[i, j][64 * (2 * p + q) : 64 * (2 * p + q) + 64] for i, j, p, q in near]
                total[s, x, y, l, 16:80] += functools.reduce(jnp.add, cell)
                side = [solved[i, j][256 + 16 * p : 272 + 16 * p] for i, j, p, q in near if q == 1]
                if side:
                    total[s, x, y, l, 80:96] += functools.reduce(jnp.add, side)
                if not upper:
                    base = [solved[i, j][288 + 16 * (2 * p + q) : 304 + 16 * (2 * p + q)] for i, j, p, q in near]
                    total[s, x, y, l, 0:16] += functools.reduce(jnp.add, base)

    def send_back(s, layers, numbers):
        for l in layers:
            for k in (1, 2):
                out_x[s, l, k - 1, 0:96] = total[s, 0, k, l].astype(BF16)
                out_x[s, l, k - 1, 96:112] = total[s, 1, k, l, 64:80].astype(BF16)
                out_y[s, l, k - 1, 0:96] = total[s, k, 0, l].astype(BF16)
                out_y[s, l, k - 1, 96:112] = total[s, k, 1, l, 80:96].astype(BF16)
            out_xy[s, l, 0:96] = total[s, 0, 0, l].astype(BF16)
            out_xy[s, l, 96:112] = total[s, 1, 0, l, 64:80].astype(BF16)
            out_xy[s, l, 112:128] = total[s, 0, 1, l, 80:96].astype(BF16)
        send(s, *numbers)

    def take_back(s, layers, numbers):
        def from_x():
            for l in layers:
                for k in (1, 2):
                    total[s, 2, k, l] += in_x[s, l, k - 1, 0:96].astype(F32)
                    total[s, 3, k, l, 64:80] += in_x[s, l, k - 1, 96:112].astype(F32)

        def from_y():
            for l in layers:
                for k in (1, 2):
                    total[s, k, 2, l] += in_y[s, l, k - 1, 0:96].astype(F32)
                    total[s, k, 3, l, 80:96] += in_y[s, l, k - 1, 96:112].astype(F32)

        def from_xy():
            for l in layers:
                total[s, 2, 2, l] += in_xy[s, l, 0:96].astype(F32)
                total[s, 3, 2, l, 64:80] += in_xy[s, l, 96:112].astype(F32)
                total[s, 2, 3, l, 80:96] += in_xy[s, l, 112:128].astype(F32)

        for number, use, then in ((numbers[1], from_y, BACK_Z_Y), (numbers[0], from_x, BACK_Z_X), (numbers[2], from_xy, None)):
            receive(s, number, use)
            if then is not None and layers == (0,):
                x, y = (1, 2) if then == BACK_Z_Y else (2, 1)
                m = BLOCK * (2 * x + y - 3)
                out_z[s, m : m + BLOCK] = total[s, x, y, 0].astype(BF16)
                send(s, then)

    def send_back_z_first(s):
        out_z[s, 0:BLOCK] = total[s, 1, 1, 0].astype(BF16)
        send(s, BACK_Z_FIRST)

    def send_back_z(s):
        out_z[s, 3 * BLOCK : 4 * BLOCK] = total[s, 2, 2, 0].astype(BF16)
        for k in (1, 2):
            m = 384 + 16 * (k - 1)
            out_z[s, m : m + 16] = total[s, 3, k, 0, 64:80].astype(BF16)
            out_z[s, m + 32 : m + 48] = total[s, k, 3, 0, 80:96].astype(BF16)
        send(s, BACK_Z)

    def take_back_z(s):
        def use():
            for x in (1, 2):
                for y in (1, 2):
                    m = BLOCK * (2 * x + y - 3)
                    total[s, x, y, 2] += in_z[s, m : m + BLOCK].astype(F32)
            for k in (1, 2):
                m = 384 + 16 * (k - 1)
                total[s, 3, k, 2, 64:80] += in_z[s, m : m + 16].astype(F32)
                total[s, k, 3, 2, 80:96] += in_z[s, m + 32 : m + 48].astype(F32)

        receive(s, BACK_Z_FIRST)
        receive(s, BACK_Z_Y)
        receive(s, BACK_Z_X)
        receive(s, BACK_Z, use)

    def clear_total(s):
        @pl.when(first_y)
        def _():
            total[s, 1:3, 1, :, 80:96] = jnp.zeros((2, 3, 16, 128), F32)

        @pl.when(first_z)
        def _():
            total[s, 1:3, 1:3, 0, 0:16] = jnp.zeros((2, 2, 16, 128), F32)

    def images(s, l):
        for x in (1, 2):
            for y in (1, 2):
                i = 2 * x + y - 3
                local = jnp.concatenate(
                    [
                        total[s, x, y, l],
                        total[s, x, y, l - 1, 0:16],
                        total[s, x + 1, y, l, 64:80],
                        total[s, x, y + 1, l, 80:96],
                    ],
                    axis=0,
                )
                upper = local.astype(BF16)
                lower = (local - upper.astype(F32)).astype(BF16)
                image = jnp.dot(high[l - 1, i], upper, preferred_element_type=F32)
                image += jnp.dot(high[l - 1, i], lower, preferred_element_type=F32)
                image += jnp.dot(low[l - 1, i], upper, preferred_element_type=F32)
                change[s, x, y, l] += image[0:96]
                change[s, x, y, l - 1, 0:16] += image[96:112]
                change[s, x + 1, y, l, 64:80] += image[112:128]
                change[s, x, y + 1, l, 80:96] += image[128:144]

    def send_images(s, l):
        if l == 2:
            for x in (1, 2):
                for y in (1, 2):
                    m = 16 * (2 * x + y - 3)
                    out_iz[s, m : m + 16] = change[s, x, y, 2, 0:16].astype(BF16)
            send(s, IMAGE_Z)
        for k in (1, 2):
            m = 16 * (k - 1)
            out_ix[s, l - 1, m : m + 16] = change[s, 3, k, l, 64:80].astype(BF16)
            out_iy[s, l - 1, m : m + 16] = change[s, k, 3, l, 80:96].astype(BF16)
        send(s, IMAGE_X + l - 1, IMAGE_Y + l - 1)

    def take_images(s, l):
        def from_x():
            for k in (0, 1):
                left[0, k, l, 64:80] -= in_ix[s, l - 1, 16 * k : 16 * k + 16].astype(F32)

        def from_y():
            for k in (0, 1):
                left[k, 0, l, 80:96] -= in_iy[s, l - 1, 16 * k : 16 * k + 16].astype(F32)

        receive(s, IMAGE_X + l - 1, from_x)
        receive(s, IMAGE_Y + l - 1, from_y)

    def take_images_z(s):
        def use():
            for x in (1, 2):
                for y in (1, 2):
                    m = 16 * (2 * x + y - 3)
                    change[s, x, y, 0, 0:16] += in_iz[s, m : m + 16].astype(F32)

        receive(s, IMAGE_Z, use)

    def update_early(s):
        for x in (1, 2):
            for y in (1, 2):
                left[x - 1, y - 1, 1] -= change[s, x, y, 1]
                left[x - 1, y - 1, 2, 16:96] -= change[s, x, y, 2, 16:96]
        clear_left()

    def update_late(s):
        for x in (1, 2):
            for y in (1, 2):
                left[x - 1, y - 1, 0, 0:16] -= change[s, x, y, 0, 0:16]
        clear_left()

    early = (EARLY_X, EARLY_Y, EARLY_XY)
    late = (LATE_X, LATE_Y, LATE_XY)
    back = (BACK_X, BACK_Y, BACK_XY)
    back2 = (BACK2_X, BACK2_Y, BACK2_XY)
    z_early = (Z_UPPER, Z_LOWER, Z_FACE)
    z_late = (Z_LAST_X, Z_LAST_Y)

    blank_total(0)
    for load in loads[1:]:
        load.wait()

    def separate(i, carry):
        x, y = i // 2, i % 2
        for k in range(5):
            width = min(128, PATCH - 128 * k)
            wide[k, :, 0:width] = pairs[x, y, :, 128 * k : 128 * k + width].astype(F32)
        for z in range(2):
            for k in range(5):
                width = min(128, PATCH - 128 * k)
                rows = wide[k, pl.ds(z, PATCH, stride=2), :].astype(BF16)
                held[x, y, z, :, 128 * k : 128 * k + width] = rows[:, 0:width]
        return carry

    lax.fori_loop(0, 4, separate, 0)
    send(0, *early)
    prepare(0, 0, 3)
    for s in range(SWEEPS):
        if s == 0:
            receive(s, Z_FIRST)
            send(s, LATE_X, LATE_XY)
            receive(s, Z_SECOND)
            send(s, LATE_Y)
            prepare(0, 3, 4)
            receive(s, Z_HALO)
            prepare(1, 0, 1)
            for number in early:
                receive(s, number)
        else:
            for number in early:
                receive(s, number)
            solve(s, 1, False)
            solve(s, 1, True)
            take_images_z(s - 1)
            update_late(s - 1)
            round_late(s)
            for number in z_early + z_late:
                receive(s, number)
            send(s, *late)
        for number in late:
            receive(s, number)
        solve(s, 0, False)
        send_back_z_first(s)
        send_back(s, (0,), back)
        solve(s, 0, True)
        if s == 0:
            prepare(1, 1, 3)
        else:
            send_back(s, (1, 2), back2)
        take_back(s, (0,), back)
        send_back_z(s)
        if s == 0:
            prepare(1, 3, 4)
            solve(s, 1, False)
            solve(s, 1, True)
            send_back(s, (1, 2), back2)
            lax.fori_loop(0, 4, elements, 0)
            blank_change()
            blank_total(1)
        take_back(s, (1, 2), back2)
        clear_total(s)
        images(s, 1)
        send_images(s, 1)
        take_back_z(s)
        clear_total(s)
        images(s, 2)
        send_images(s, 2)
        update_early(s)
        if s < SWEEPS - 1:
            round_early(s + 1)
            send(s + 1, *z_early)
        take_images(s, 1)
        take_images(s, 2)
        clear_left()
        if s < SWEEPS - 1:
            round_faces(s + 1)
            send(s + 1, *z_late)
            send(s + 1, *early)

    for x in range(2):
        for y in range(2):
            for z in range(2):
                block = total[0, x + 1, y + 1, z + 1] + total[1, x + 1, y + 1, z + 1]
                solution_ref[x, y, 0:63, z, :] = block[16:79]
                solution_ref[x, y, 63:72, z, :] = block[80:89]
                lower = total[0, x + 1, y + 1, z, 0:16] + total[1, x + 1, y + 1, z, 0:16]
                solution_ref[x, y, 72:81, z, :] = lower[0:9]
                residual_ref[x, y, 0:63, z, :] = left[x, y, z + 1, 16:79]
                residual_ref[x, y, 63:72, z, :] = left[x, y, z + 1, 80:89]
    take_images_z(SWEEPS - 1)
    update_late(SWEEPS - 1)
    for x in range(2):
        for y in range(2):
            for z in range(2):
                residual_ref[x, y, 72:81, z, :] = left[x, y, z, 0:9]

    for copy, sends, _ in routes.values():
        if_(sends, copy.wait_send)


def body(residual_start, patch_inverse, patch_order, element_matrix, face_order):
    swapped = lambda value: jnp.transpose(value, (0, 1, 3, 2, 4))
    residual_start = swapped(residual_start)
    shape = jax.ShapeDtypeStruct(residual_start.shape, F32)
    vmem = pl.BlockSpec(memory_space=pltpu.VMEM)
    total, left = pl.pallas_call(
        kernel,
        out_shape=(shape, shape),
        in_specs=[pl.BlockSpec(memory_space=pltpu.HBM)] * 5,
        out_specs=(vmem, vmem),
        scratch_shapes=[
            pltpu.VMEM(residual_start.shape, F32),
            pltpu.VMEM(patch_order.shape, jnp.int32),
            pltpu.VMEM((2, 2, LOCAL, 2, LOCAL), F32),
            pltpu.VMEM((2, 2, 6, 2, FACE), jnp.int32),
            pltpu.VMEM((2, 2, 2 * PATCH, PATCH), BF16),
            pltpu.VMEM((5, 2 * PATCH, 128), F32),
            pltpu.VMEM((2, 2, 2, PATCH, PATCH), BF16),
            pltpu.VMEM((2, 4, STAR, STAR), BF16),
            pltpu.VMEM((2, 4, WIDE, WIDE), BF16),
            pltpu.VMEM((2, 4, WIDE, WIDE), BF16),
            pltpu.VMEM((SWEEPS, 3, 3, 3, BLOCK, 128), BF16),
            pltpu.VMEM((SWEEPS, 4, 4, 3, BLOCK, 128), F32),
            pltpu.VMEM((SWEEPS, 4, 4, 3, BLOCK, 128), F32),
            pltpu.VMEM((2, 2, 3, BLOCK, 128), F32),
            pltpu.VMEM((SWEEPS, 3, 2, 112, 128), BF16),
            pltpu.VMEM((SWEEPS, 3, 2, 112, 128), BF16),
            pltpu.VMEM((SWEEPS, 3, 128, 128), BF16),
            pltpu.VMEM((SWEEPS, 3, 2, 112, 128), BF16),
            pltpu.VMEM((SWEEPS, 3, 2, 112, 128), BF16),
            pltpu.VMEM((SWEEPS, 3, 128, 128), BF16),
            pltpu.VMEM((SWEEPS, 448, 128), BF16),
            pltpu.VMEM((SWEEPS, 448, 128), BF16),
            pltpu.VMEM((SWEEPS, 2, 32, 128), BF16),
            pltpu.VMEM((SWEEPS, 2, 32, 128), BF16),
            pltpu.VMEM((SWEEPS, 64, 128), BF16),
            pltpu.VMEM((SWEEPS, 2, 32, 128), BF16),
            pltpu.VMEM((SWEEPS, 2, 32, 128), BF16),
            pltpu.VMEM((SWEEPS, 64, 128), BF16),
            pltpu.SemaphoreType.DMA((8,)),
            pltpu.SemaphoreType.DMA((SWEEPS, COPIES)),
            pltpu.SemaphoreType.DMA((SWEEPS, COPIES)),
        ],
        compiler_params=pltpu.CompilerParams(
            collective_id=0, has_side_effects=True, vmem_limit_bytes=60 * 1024 * 1024
        ),
    )(residual_start, swapped(patch_inverse), patch_order, swapped(element_matrix), swapped(face_order))

    def finish(first, second, first_out, second_out, sem):
        copies = [
            pltpu.make_async_copy(first, first_out, sem.at[0]),
            pltpu.make_async_copy(second, second_out, sem.at[1]),
        ]
        for copy in copies:
            copy.start()
        for copy in copies:
            copy.wait()

    total, left = pl.pallas_call(
        finish,
        out_shape=(shape, shape),
        in_specs=[vmem, vmem],
        out_specs=(pl.BlockSpec(memory_space=pltpu.HBM), pl.BlockSpec(memory_space=pltpu.HBM)),
        scratch_shapes=[pltpu.SemaphoreType.DMA((2,))],
    )(total, left)
    return swapped(total), swapped(left)


def solution(mesh):
    return jax.shard_map(
        body,
        mesh=mesh,
        in_specs=(
            P("gx", "gy", "gz", None, None),
            P("gx", "gy", "gz", None, None),
            P("gx", "gy", "gz", None),
            P("gx", "gy", "gz", None, None),
            P("gx", "gy", "gz", None, None),
        ),
        out_specs=(P("gx", "gy", "gz", None, None), P("gx", "gy", "gz", None, None)),
        check_vma=False,
    )
```

```python
import functools

import jax
import jax.numpy as jnp
from jax import lax
from jax.experimental import pallas as pl
from jax.experimental.pallas import tpu as pltpu
from jax.sharding import PartitionSpec as P

INNER = 54
FACE = 9
SWEEPS = 2
PATCH = 540
LOCAL = 108
STAR = 640
WIDE = 144
BLOCK = 96
MESH = pl.DeviceIdType.MESH
F32 = jnp.float32
BF16 = jnp.bfloat16

Z_HALO = 0
EARLY_X, EARLY_Y, EARLY_XY = 1, 2, 3
LATE_X, LATE_Y, LATE_XY = 4, 5, 6
BACK_X, BACK_Y, BACK_XY = 7, 8, 9
BACK2_X, BACK2_Y, BACK2_XY = 10, 11, 12
BACK_Z = 13
IMAGE_X, IMAGE_Y = 14, 16
IMAGE_Z = 18
Z_UPPER, Z_LOWER, Z_FACE, Z_LAST_X, Z_LAST_Y = 19, 20, 21, 22, 23
BACK_Z_FIRST, BACK_Z_Y, BACK_Z_X = 24, 25, 26
Z_FIRST, Z_SECOND = 27, 28
COPIES = 29

CELL_ROWS = [64 * (m // 2) + 352 * (m % 2) for m in range(8)]
Y_ROWS = [256 + 16 * (g // 2) + (608 - 256) * (g % 2) for g in range(4)]
Z_ROWS = [288 + 16 * h for h in range(4)]
LOWER = 352
SEGMENTS = (
    [(INNER * m, CELL_ROWS[m]) for m in range(8)]
    + [(8 * INNER + FACE * f, CELL_ROWS[4 + f] + INNER) for f in range(4)]
    + [(8 * INNER + FACE * (4 + g), Y_ROWS[g]) for g in range(4)]
    + [(8 * INNER + FACE * (8 + h), Z_ROWS[h]) for h in range(4)]
)


def star_rows(order):
    place, shift = order, 0
    for first, row in SEGMENTS:
        step = row - first - shift
        shift += step
        if step:
            place = place + step * (order >= first).astype(jnp.int32)
    return place


def kernel(
    start_any, inverse_any, order_any, matrix_any, faces_any,
    solution_ref, residual_ref,
    start_ref, order_ref, matrix_ref, faces_ref, pairs, wide, held, stars, high, low, rim, total, change, left,
    out_x, out_y, out_xy, in_x, in_y, in_xy, out_z, in_z,
    out_ix, out_iy, out_iz, in_ix, in_iy, in_iz,
    load_sem, send_sem, recv_sem,
):
    gx, gy, gz = lax.axis_index("gx"), lax.axis_index("gy"), lax.axis_index("gz")
    count_x, count_y, count_z = lax.axis_size("gx"), lax.axis_size("gy"), lax.axis_size("gz")
    up_x, down_x = lax.rem(gx + 1, count_x), lax.rem(gx + count_x - 1, count_x)
    first_y, last_y = gy == 0, gy == count_y - 1
    first_z, last_z = gz == 0, gz == count_z - 1
    not_first_y, not_last_y = gy > 0, gy < count_y - 1
    not_first_z, not_last_z = gz > 0, gz < count_z - 1

    barrier = pltpu.get_barrier_semaphore()

    def greet(device):
        pl.semaphore_signal(barrier, inc=1, device_id=device, device_id_type=MESH)

    greet((up_x, gy, gz))
    greet((down_x, gy, gz))

    @pl.when(not_last_y)
    def _():
        greet((gx, gy + 1, gz))
        greet((up_x, gy + 1, gz))

    @pl.when(not_first_y)
    def _():
        greet((gx, gy - 1, gz))
        greet((down_x, gy - 1, gz))

    @pl.when(not_last_z)
    def _():
        greet((gx, gy, gz + 1))

    @pl.when(not_first_z)
    def _():
        greet((gx, gy, gz - 1))

    inverses = inverse_any.reshape(2, 2, 2 * PATCH, PATCH)
    loads = [pltpu.make_async_copy(start_any, start_ref, load_sem.at[0])]
    for x in range(2):
        for y in range(2):
            loads.append(pltpu.make_async_copy(inverses.at[x, y], pairs.at[x, y], load_sem.at[1 + 2 * x + y]))
    loads.append(pltpu.make_async_copy(order_any, order_ref, load_sem.at[5]))
    loads.append(pltpu.make_async_copy(matrix_any, matrix_ref, load_sem.at[6]))
    loads.append(pltpu.make_async_copy(faces_any, faces_ref, load_sem.at[7]))
    for load in loads:
        load.start()

    def blank(x, y, layers, rows):
        for s in range(SWEEPS):
            for l in layers:
                rim[s, x, y, l, rows] = jnp.zeros((rows.stop - rows.start, 128), BF16)

    for x in (1, 2):
        for y in (1, 2):
            blank(x, y, (2,), slice(0, 16))

    @pl.when(first_y)
    def _():
        for x in range(3):
            blank(x, 0, (0, 1, 2), slice(0, 96))

    @pl.when(first_z)
    def _():
        for x in (1, 2):
            for y in (1, 2):
                blank(x, y, (0,), slice(16, 96))

    always = None
    routes = {}

    def route(s, number, src, dst, device, sends, receives):
        copy = pltpu.make_async_remote_copy(
            src_ref=src, dst_ref=dst, send_sem=send_sem.at[s, number], recv_sem=recv_sem.at[s, number],
            device_id=device, device_id_type=MESH,
        )
        routes[s, number] = (copy, sends, receives)

    upper_y, lower_y = gy + 1, gy - 1
    for s in range(SWEEPS):
        here = rim.at[s]
        parts = (
            (Z_FIRST, slice(2, 3), slice(1, 3), slice(16, 96)),
            (Z_SECOND, slice(1, 2), slice(2, 3), slice(16, 96)),
            (Z_HALO, slice(1, 2), slice(1, 2), slice(16, 96)),
        )
        if s > 0:
            parts = (
                (Z_UPPER, slice(2, 3), slice(1, 3), slice(16, 80)),
                (Z_LOWER, slice(1, 2), slice(1, 3), slice(16, 64)),
                (Z_FACE, slice(1, 3), slice(2, 3), slice(80, 96)),
                (Z_LAST_X, slice(1, 2), slice(1, 3), slice(64, 80)),
                (Z_LAST_Y, slice(1, 3), slice(1, 2), slice(80, 96)),
            )
        for number, x, y, rows in parts:
            route(s, number, here.at[x, y, 2, rows], here.at[x, y, 0, rows], (gx, gy, gz + 1),
                  not_last_z, not_first_z)
        for x, y, xy, layers in ((EARLY_X, EARLY_Y, EARLY_XY, slice(1, 3)), (LATE_X, LATE_Y, LATE_XY, slice(0, 1))):
            route(s, x, here.at[2, 1:3, layers], here.at[0, 1:3, layers], (up_x, gy, gz), always, always)
            route(s, y, here.at[1:3, 2, layers], here.at[1:3, 0, layers], (gx, upper_y, gz), not_last_y, not_first_y)
            route(s, xy, here.at[2, 2, layers], here.at[0, 0, layers], (up_x, upper_y, gz), not_last_y, not_first_y)
        for x, y, xy, layers in ((BACK_X, BACK_Y, BACK_XY, slice(0, 1)), (BACK2_X, BACK2_Y, BACK2_XY, slice(1, 3))):
            route(s, x, out_x.at[s, layers], in_x.at[s, layers], (down_x, gy, gz), always, always)
            route(s, y, out_y.at[s, layers], in_y.at[s, layers], (gx, lower_y, gz), not_first_y, not_last_y)
            route(s, xy, out_xy.at[s, layers], in_xy.at[s, layers], (down_x, lower_y, gz), not_first_y, not_last_y)
        for number, rows in (
            (BACK_Z_FIRST, slice(0, 96)),
            (BACK_Z_Y, slice(96, 192)),
            (BACK_Z_X, slice(192, 288)),
            (BACK_Z, slice(288, 448)),
        ):
            route(s, number, out_z.at[s, rows], in_z.at[s, rows], (gx, gy, gz - 1), not_first_z, not_last_z)
        for l in (0, 1):
            route(s, IMAGE_X + l, out_ix.at[s, l], in_ix.at[s, l], (up_x, gy, gz), always, always)
            route(s, IMAGE_Y + l, out_iy.at[s, l], in_iy.at[s, l], (gx, upper_y, gz), not_last_y, not_first_y)
        route(s, IMAGE_Z, out_iz.at[s], in_iz.at[s], (gx, gy, gz + 1), not_last_z, not_first_z)

    def if_(flag, action):
        if flag is None:
            action()
        else:
            pl.when(flag)(action)

    def send(s, *numbers):
        for number in numbers:
            copy, sends, _ = routes[s, number]
            if_(sends, copy.start)

    def receive(s, number, use=None):
        copy, _, receives = routes[s, number]

        def action():
            copy.wait_recv()
            if use is not None:
                use()

        if_(receives, action)

    def clear_left():
        @pl.when(first_y)
        def _():
            left[:, 0, :, 80:96] = jnp.zeros((2, 3, 16, 128), F32)

        @pl.when(first_z)
        def _():
            left[:, :, 0, 0:16] = jnp.zeros((2, 2, 16, 128), F32)

    left[...] = jnp.zeros_like(left)
    loads[0].wait()
    for x in range(2):
        for y in range(2):
            for z in range(2):
                left[x, y, z + 1, 16:79] = start_ref[x, y, 0:63, z, :]
                left[x, y, z + 1, 80:89] = start_ref[x, y, 63:72, z, :]
                left[x, y, z, 0:9] = start_ref[x, y, 72:81, z, :]
    clear_left()

    def round_early(s):
        for x in range(2):
            for y in range(2):
                rim[s, x + 1, y + 1, 1] = left[x, y, 1].astype(BF16)
                rim[s, x + 1, y + 1, 2, 16:96] = left[x, y, 2, 16:96].astype(BF16)

    def round_late(s):
        for x in range(2):
            for y in range(2):
                rim[s, x + 1, y + 1, 0, 0:16] = left[x, y, 0, 0:16].astype(BF16)

    def round_faces(s):
        for l in (1, 2):
            for k in range(2):
                rim[s, 1, k + 1, l, 64:80] = left[0, k, l, 64:80].astype(BF16)
                rim[s, k + 1, 1, l, 80:96] = left[k, 0, l, 80:96].astype(BF16)

    round_early(0)
    round_late(0)

    met = 2 + 2 * not_last_y.astype(jnp.int32) + 2 * not_first_y.astype(jnp.int32)
    met = met + not_last_z.astype(jnp.int32) + not_first_z.astype(jnp.int32)
    pl.semaphore_wait(barrier, met)

    send(0, Z_FIRST, Z_SECOND, Z_HALO)

    def blank_total(s):
        def one(i, carry):
            total[s, i // 12, (i // 3) % 4, i % 3] = jnp.zeros((BLOCK, 128), F32)
            return carry

        lax.fori_loop(0, 48, one, 0)

    def blank_change(s):
        def one(i, carry):
            change[s, i // 12, (i // 3) % 4, i % 3] = jnp.zeros((BLOCK, 128), F32)
            return carry

        lax.fori_loop(0, 48, one, 0)

    dims_nt = (((1,), (1,)), ((), ()))

    lane = lax.broadcasted_iota(jnp.int32, (1, LOCAL), 1)
    face = sum((lane >= INNER + FACE * f).astype(jnp.int32) for f in range(1, 6))
    slot = lane - INNER - FACE * face
    spread = (lax.broadcasted_iota(jnp.int32, (FACE, LOCAL), 0) == slot).astype(F32)
    own_face = (lax.broadcasted_iota(jnp.int32, (6, LOCAL), 0) == face) & (lane >= INNER)
    base = jnp.where(lane < INNER, 16 + lane, 0)
    for f, offset in enumerate((70, 118, 80, 128, 96, 0)):
        base = base + jnp.where((lane >= INNER) & (face == f), offset, 0)
    base = base.astype(F32)
    wide_rows = lax.broadcasted_iota(jnp.int32, (WIDE, LOCAL), 0).astype(F32)

    def element(i, z):
        x, y = i // 2, i % 2
        listed = jnp.dot(faces_ref[x, y, :, z, :].astype(F32).astype(BF16), spread.astype(BF16), preferred_element_type=F32)
        place = base + jnp.sum(jnp.where(own_face, listed, 0.0), axis=0, keepdims=True)
        pick = jnp.where(wide_rows == place, 1.0, 0.0).astype(BF16)
        matrix = matrix_ref[x, y, :, z, :]
        upper = matrix.astype(BF16)
        lower = (matrix - upper.astype(F32)).astype(BF16)
        for part, ref in ((upper, high), (lower, low)):
            rows = jnp.dot(pick, part, preferred_element_type=F32).astype(BF16)
            ref[z, i] = lax.dot_general(rows, pick, dims_nt, preferred_element_type=F32).astype(BF16)

    def elements(i, carry):
        element(i, 0)
        element(i, 1)
        return carry


    star_iota = lax.broadcasted_iota(jnp.int32, (STAR, PATCH), 0)

    def prepare(c, first, last):
        def vertex(i, carry):
            x, y = i // 2, i % 2
            place = star_rows(order_ref[x, y, c : c + 1, :])
            pick = jnp.where(star_iota == place, 1.0, 0.0).astype(BF16)
            rows = jnp.dot(pick, held[x, y, c], preferred_element_type=F32).astype(BF16)
            stars[c, i] = lax.dot_general(rows, pick, dims_nt, preferred_element_type=F32).astype(BF16)
            return carry

        lax.fori_loop(first, last, vertex, 0)

    def star(s, c, x, y):
        pieces = []
        for p in (0, 1):
            for q in (0, 1):
                pieces.append(rim[s, x + p, y + q, c, 16:80])
        for p in (0, 1):
            pieces.append(rim[s, x + p, y + 1, c, 80:96])
        for p in (0, 1):
            for q in (0, 1):
                pieces.append(rim[s, x + p, y + q, c, 0:16])
        for p in (0, 1):
            for q in (0, 1):
                pieces.append(rim[s, x + p, y + q, c + 1, 16:80])
        for p in (0, 1):
            pieces.append(rim[s, x + p, y + 1, c + 1, 80:96])
        return jnp.concatenate(pieces, axis=0)

    def solve(s, c, upper):
        first, last = (LOWER, STAR) if upper else (0, LOWER)
        solved = {}
        for x in (0, 1):
            for y in (0, 1):
                solved[x, y] = jnp.dot(stars[c, 2 * x + y, first:last], star(s, c, x, y), preferred_element_type=F32)
        l = c + 1 if upper else c
        for x in range(3):
            for y in range(3):
                near = [(x - p, y - q, p, q) for p in (0, 1) for q in (0, 1) if 0 <= x - p < 2 and 0 <= y - q < 2]
                cell = [solved[i, j][64 * (2 * p + q) : 64 * (2 * p + q) + 64] for i, j, p, q in near]
                total[s, x, y, l, 16:80] += functools.reduce(jnp.add, cell)
                side = [solved[i, j][256 + 16 * p : 272 + 16 * p] for i, j, p, q in near if q == 1]
                if side:
                    total[s, x, y, l, 80:96] += functools.reduce(jnp.add, side)
                if not upper:
                    base = [solved[i, j][288 + 16 * (2 * p + q) : 304 + 16 * (2 * p + q)] for i, j, p, q in near]
                    total[s, x, y, l, 0:16] += functools.reduce(jnp.add, base)

    def send_back(s, layers, numbers):
        for l in layers:
            for k in (1, 2):
                out_x[s, l, k - 1, 0:96] = total[s, 0, k, l].astype(BF16)
                out_x[s, l, k - 1, 96:112] = total[s, 1, k, l, 64:80].astype(BF16)
                out_y[s, l, k - 1, 0:96] = total[s, k, 0, l].astype(BF16)
                out_y[s, l, k - 1, 96:112] = total[s, k, 1, l, 80:96].astype(BF16)
            out_xy[s, l, 0:96] = total[s, 0, 0, l].astype(BF16)
            out_xy[s, l, 96:112] = total[s, 1, 0, l, 64:80].astype(BF16)
            out_xy[s, l, 112:128] = total[s, 0, 1, l, 80:96].astype(BF16)
        send(s, *numbers)

    def take_back(s, layers, numbers):
        def from_x():
            for l in layers:
                for k in (1, 2):
                    total[s, 2, k, l] += in_x[s, l, k - 1, 0:96].astype(F32)
                    total[s, 3, k, l, 64:80] += in_x[s, l, k - 1, 96:112].astype(F32)

        def from_y():
            for l in layers:
                for k in (1, 2):
                    total[s, k, 2, l] += in_y[s, l, k - 1, 0:96].astype(F32)
                    total[s, k, 3, l, 80:96] += in_y[s, l, k - 1, 96:112].astype(F32)

        def from_xy():
            for l in layers:
                total[s, 2, 2, l] += in_xy[s, l, 0:96].astype(F32)
                total[s, 3, 2, l, 64:80] += in_xy[s, l, 96:112].astype(F32)
                total[s, 2, 3, l, 80:96] += in_xy[s, l, 112:128].astype(F32)

        for number, use, then in ((numbers[1], from_y, BACK_Z_Y), (numbers[0], from_x, BACK_Z_X), (numbers[2], from_xy, None)):
            receive(s, number, use)
            if then is not None and layers == (0,):
                x, y = (1, 2) if then == BACK_Z_Y else (2, 1)
                m = BLOCK * (2 * x + y - 3)
                out_z[s, m : m + BLOCK] = total[s, x, y, 0].astype(BF16)
                send(s, then)

    def send_back_z_first(s):
        out_z[s, 0:BLOCK] = total[s, 1, 1, 0].astype(BF16)
        send(s, BACK_Z_FIRST)

    def send_back_z(s):
        out_z[s, 3 * BLOCK : 4 * BLOCK] = total[s, 2, 2, 0].astype(BF16)
        for k in (1, 2):
            m = 384 + 16 * (k - 1)
            out_z[s, m : m + 16] = total[s, 3, k, 0, 64:80].astype(BF16)
            out_z[s, m + 32 : m + 48] = total[s, k, 3, 0, 80:96].astype(BF16)
        send(s, BACK_Z)

    def take_back_z(s):
        def use():
            for x in (1, 2):
                for y in (1, 2):
                    m = BLOCK * (2 * x + y - 3)
                    total[s, x, y, 2] += in_z[s, m : m + BLOCK].astype(F32)
            for k in (1, 2):
                m = 384 + 16 * (k - 1)
                total[s, 3, k, 2, 64:80] += in_z[s, m : m + 16].astype(F32)
                total[s, k, 3, 2, 80:96] += in_z[s, m + 32 : m + 48].astype(F32)

        receive(s, BACK_Z_FIRST)
        receive(s, BACK_Z_Y)
        receive(s, BACK_Z_X)
        receive(s, BACK_Z, use)

    def clear_total(s):
        @pl.when(first_y)
        def _():
            total[s, 1:3, 1, :, 80:96] = jnp.zeros((2, 3, 16, 128), F32)

        @pl.when(first_z)
        def _():
            total[s, 1:3, 1:3, 0, 0:16] = jnp.zeros((2, 2, 16, 128), F32)

    def images(s, l):
        for x in (1, 2):
            for y in (1, 2):
                i = 2 * x + y - 3
                local = jnp.concatenate(
                    [
                        total[s, x, y, l],
                        total[s, x, y, l - 1, 0:16],
                        total[s, x + 1, y, l, 64:80],
                        total[s, x, y + 1, l, 80:96],
                    ],
                    axis=0,
                )
                upper = local.astype(BF16)
                lower = (local - upper.astype(F32)).astype(BF16)
                image = jnp.dot(high[l - 1, i], upper, preferred_element_type=F32)
                image += jnp.dot(high[l - 1, i], lower, preferred_element_type=F32)
                image += jnp.dot(low[l - 1, i], upper, preferred_element_type=F32)
                change[s, x, y, l] += image[0:96]
                change[s, x, y, l - 1, 0:16] += image[96:112]
                change[s, x + 1, y, l, 64:80] += image[112:128]
                change[s, x, y + 1, l, 80:96] += image[128:144]

    def send_images(s, l):
        if l == 2:
            for x in (1, 2):
                for y in (1, 2):
                    m = 16 * (2 * x + y - 3)
                    out_iz[s, m : m + 16] = change[s, x, y, 2, 0:16].astype(BF16)
            send(s, IMAGE_Z)
        for k in (1, 2):
            m = 16 * (k - 1)
            out_ix[s, l - 1, m : m + 16] = change[s, 3, k, l, 64:80].astype(BF16)
            out_iy[s, l - 1, m : m + 16] = change[s, k, 3, l, 80:96].astype(BF16)
        send(s, IMAGE_X + l - 1, IMAGE_Y + l - 1)

    def take_images(s, l):
        def from_x():
            for k in (0, 1):
                left[0, k, l, 64:80] -= in_ix[s, l - 1, 16 * k : 16 * k + 16].astype(F32)

        def from_y():
            for k in (0, 1):
                left[k, 0, l, 80:96] -= in_iy[s, l - 1, 16 * k : 16 * k + 16].astype(F32)

        receive(s, IMAGE_X + l - 1, from_x)
        receive(s, IMAGE_Y + l - 1, from_y)

    def take_images_z(s):
        def use():
            for x in (1, 2):
                for y in (1, 2):
                    m = 16 * (2 * x + y - 3)
                    change[s, x, y, 0, 0:16] += in_iz[s, m : m + 16].astype(F32)

        receive(s, IMAGE_Z, use)

    def update_early(s):
        for x in (1, 2):
            for y in (1, 2):
                left[x - 1, y - 1, 1] -= change[s, x, y, 1]
                left[x - 1, y - 1, 2, 16:96] -= change[s, x, y, 2, 16:96]
        clear_left()

    def update_late(s):
        for x in (1, 2):
            for y in (1, 2):
                left[x - 1, y - 1, 0, 0:16] -= change[s, x, y, 0, 0:16]
        clear_left()

    def write_early():
        for x in range(2):
            for y in range(2):
                for z in range(2):
                    block = total[0, x + 1, y + 1, z + 1] + total[1, x + 1, y + 1, z + 1]
                    solution_ref[x, y, 0:63, z, :] = block[16:79]
                    solution_ref[x, y, 63:72, z, :] = block[80:89]
                    lower = total[0, x + 1, y + 1, z, 0:16] + total[1, x + 1, y + 1, z, 0:16]
                    solution_ref[x, y, 72:81, z, :] = lower[0:9]
                    residual_ref[x, y, 0:63, z, :] = left[x, y, z + 1, 16:79]
                    residual_ref[x, y, 63:72, z, :] = left[x, y, z + 1, 80:89]
                residual_ref[x, y, 72:81, 1, :] = left[x, y, 1, 0:9]

    early = (EARLY_X, EARLY_Y, EARLY_XY)
    late = (LATE_X, LATE_Y, LATE_XY)
    back = (BACK_X, BACK_Y, BACK_XY)
    back2 = (BACK2_X, BACK2_Y, BACK2_XY)
    z_early = (Z_UPPER, Z_LOWER, Z_FACE)
    z_late = (Z_LAST_X, Z_LAST_Y)

    blank_total(0)
    for load in loads[1:]:
        load.wait()

    def separate(i, carry):
        x, y = i // 2, i % 2
        for k in range(5):
            width = min(128, PATCH - 128 * k)
            wide[k, :, 0:width] = pairs[x, y, :, 128 * k : 128 * k + width].astype(F32)
        for z in range(2):
            for k in range(5):
                width = min(128, PATCH - 128 * k)
                rows = wide[k, pl.ds(z, PATCH, stride=2), :].astype(BF16)
                held[x, y, z, :, 128 * k : 128 * k + width] = rows[:, 0:width]
        return carry

    lax.fori_loop(0, 4, separate, 0)
    send(0, *early)
    prepare(0, 0, 3)
    for s in range(SWEEPS):
        if s == 0:
            receive(s, Z_FIRST)
            send(s, LATE_X, LATE_XY)
            receive(s, Z_SECOND)
            send(s, LATE_Y)
            prepare(0, 3, 4)
            receive(s, Z_HALO)
            prepare(1, 0, 1)
            for number in early:
                receive(s, number)
        else:
            take_images_z(s - 1)
            update_late(s - 1)
            round_late(s)
            for number in z_early + z_late:
                receive(s, number)
            send(s, *late)
            for number in early:
                receive(s, number)
            solve(s, 1, False)
            solve(s, 1, True)
        for number in late:
            receive(s, number)
        solve(s, 0, False)
        send_back_z_first(s)
        send_back(s, (0,), back)
        solve(s, 0, True)
        if s == 0:
            prepare(1, 1, 3)
        else:
            send_back(s, (1, 2), back2)
        take_back(s, (0,), back)
        send_back_z(s)
        if s == 0:
            prepare(1, 3, 4)
            solve(s, 1, False)
            solve(s, 1, True)
            send_back(s, (1, 2), back2)
            lax.fori_loop(0, 4, elements, 0)
            blank_change(0)
        take_back(s, (1, 2), back2)
        clear_total(s)
        images(s, 1)
        send_images(s, 1)
        take_back_z(s)
        clear_total(s)
        images(s, 2)
        send_images(s, 2)
        update_early(s)
        if s < SWEEPS - 1:
            round_early(s + 1)
            send(s + 1, *z_early)
            blank_total(s + 1)
            blank_change(s + 1)
        else:
            write_early()
        take_images(s, 1)
        take_images(s, 2)
        clear_left()
        if s < SWEEPS - 1:
            round_faces(s + 1)
            send(s + 1, *z_late)
            send(s + 1, *early)

    for z in range(2):
        for k in range(2):
            residual_ref[0, k, 54:63, z, :] = left[0, k, z + 1, 70:79]
            residual_ref[k, 0, 63:72, z, :] = left[k, 0, z + 1, 80:89]
    take_images_z(SWEEPS - 1)
    update_late(SWEEPS - 1)
    for x in range(2):
        for y in range(2):
            residual_ref[x, y, 72:81, 0, :] = left[x, y, 0, 0:9]

    for copy, sends, _ in routes.values():
        if_(sends, copy.wait_send)


def body(residual_start, patch_inverse, patch_order, element_matrix, face_order):
    swapped = lambda value: jnp.transpose(value, (0, 1, 3, 2, 4))
    residual_start = swapped(residual_start)
    shape = jax.ShapeDtypeStruct(residual_start.shape, F32)
    vmem = pl.BlockSpec(memory_space=pltpu.VMEM)
    total, left = pl.pallas_call(
        kernel,
        out_shape=(shape, shape),
        in_specs=[pl.BlockSpec(memory_space=pltpu.HBM)] * 5,
        out_specs=(vmem, vmem),
        scratch_shapes=[
            pltpu.VMEM(residual_start.shape, F32),
            pltpu.VMEM(patch_order.shape, jnp.int32),
            pltpu.VMEM((2, 2, LOCAL, 2, LOCAL), F32),
            pltpu.VMEM((2, 2, 6, 2, FACE), jnp.int32),
            pltpu.VMEM((2, 2, 2 * PATCH, PATCH), BF16),
            pltpu.VMEM((5, 2 * PATCH, 128), F32),
            pltpu.VMEM((2, 2, 2, PATCH, PATCH), BF16),
            pltpu.VMEM((2, 4, STAR, STAR), BF16),
            pltpu.VMEM((2, 4, WIDE, WIDE), BF16),
            pltpu.VMEM((2, 4, WIDE, WIDE), BF16),
            pltpu.VMEM((SWEEPS, 3, 3, 3, BLOCK, 128), BF16),
            pltpu.VMEM((SWEEPS, 4, 4, 3, BLOCK, 128), F32),
            pltpu.VMEM((SWEEPS, 4, 4, 3, BLOCK, 128), F32),
            pltpu.VMEM((2, 2, 3, BLOCK, 128), F32),
            pltpu.VMEM((SWEEPS, 3, 2, 112, 128), BF16),
            pltpu.VMEM((SWEEPS, 3, 2, 112, 128), BF16),
            pltpu.VMEM((SWEEPS, 3, 128, 128), BF16),
            pltpu.VMEM((SWEEPS, 3, 2, 112, 128), BF16),
            pltpu.VMEM((SWEEPS, 3, 2, 112, 128), BF16),
            pltpu.VMEM((SWEEPS, 3, 128, 128), BF16),
            pltpu.VMEM((SWEEPS, 448, 128), BF16),
            pltpu.VMEM((SWEEPS, 448, 128), BF16),
            pltpu.VMEM((SWEEPS, 2, 32, 128), BF16),
            pltpu.VMEM((SWEEPS, 2, 32, 128), BF16),
            pltpu.VMEM((SWEEPS, 64, 128), BF16),
            pltpu.VMEM((SWEEPS, 2, 32, 128), BF16),
            pltpu.VMEM((SWEEPS, 2, 32, 128), BF16),
            pltpu.VMEM((SWEEPS, 64, 128), BF16),
            pltpu.SemaphoreType.DMA((8,)),
            pltpu.SemaphoreType.DMA((SWEEPS, COPIES)),
            pltpu.SemaphoreType.DMA((SWEEPS, COPIES)),
        ],
        compiler_params=pltpu.CompilerParams(
            collective_id=0, has_side_effects=True, vmem_limit_bytes=60 * 1024 * 1024
        ),
    )(residual_start, swapped(patch_inverse), patch_order, swapped(element_matrix), swapped(face_order))

    def finish(first, second, first_out, second_out, sem):
        copies = [
            pltpu.make_async_copy(first, first_out, sem.at[0]),
            pltpu.make_async_copy(second, second_out, sem.at[1]),
        ]
        for copy in copies:
            copy.start()
        for copy in copies:
            copy.wait()

    total, left = pl.pallas_call(
        finish,
        out_shape=(shape, shape),
        in_specs=[vmem, vmem],
        out_specs=(pl.BlockSpec(memory_space=pltpu.HBM), pl.BlockSpec(memory_space=pltpu.HBM)),
        scratch_shapes=[pltpu.SemaphoreType.DMA((2,))],
    )(total, left)
    return swapped(total), swapped(left)


def solution(mesh):
    return jax.shard_map(
        body,
        mesh=mesh,
        in_specs=(
            P("gx", "gy", "gz", None, None),
            P("gx", "gy", "gz", None, None),
            P("gx", "gy", "gz", None),
            P("gx", "gy", "gz", None, None),
            P("gx", "gy", "gz", None, None),
        ),
        out_specs=(P("gx", "gy", "gz", None, None), P("gx", "gy", "gz", None, None)),
        check_vma=False,
    )
```

```python
import functools

import jax
import jax.numpy as jnp
from jax import lax
from jax.experimental import pallas as pl
from jax.experimental.pallas import tpu as pltpu
from jax.sharding import PartitionSpec as P

INNER = 54
FACE = 9
SWEEPS = 2
PATCH = 540
LOCAL = 108
STAR = 640
WIDE = 144
BLOCK = 96
MESH = pl.DeviceIdType.MESH
F32 = jnp.float32
BF16 = jnp.bfloat16

Z_HALO = 0
EARLY_X, EARLY_Y, EARLY_XY = 1, 2, 3
LATE_X, LATE_Y, LATE_XY = 4, 5, 6
BACK_X, BACK_Y, BACK_XY = 7, 8, 9
BACK2_X, BACK2_Y, BACK2_XY = 10, 11, 12
BACK_Z = 13
IMAGE_X, IMAGE_Y = 14, 16
IMAGE_Z = 18
Z_UPPER, Z_LOWER, Z_FACE, Z_LAST_X, Z_LAST_Y = 19, 20, 21, 22, 23
BACK_Z_FIRST, BACK_Z_Y, BACK_Z_X = 24, 25, 26
Z_FIRST, Z_SECOND = 27, 28
COPIES = 29

CELL_ROWS = [64 * (m // 2) + 352 * (m % 2) for m in range(8)]
Y_ROWS = [256 + 16 * (g // 2) + (608 - 256) * (g % 2) for g in range(4)]
Z_ROWS = [288 + 16 * h for h in range(4)]
LOWER = 352
SEGMENTS = (
    [(INNER * m, CELL_ROWS[m]) for m in range(8)]
    + [(8 * INNER + FACE * f, CELL_ROWS[4 + f] + INNER) for f in range(4)]
    + [(8 * INNER + FACE * (4 + g), Y_ROWS[g]) for g in range(4)]
    + [(8 * INNER + FACE * (8 + h), Z_ROWS[h]) for h in range(4)]
)


def star_rows(order):
    place, shift = order, 0
    for first, row in SEGMENTS:
        step = row - first - shift
        shift += step
        if step:
            place = place + step * (order >= first).astype(jnp.int32)
    return place


def kernel(
    start_any, inverse_any, order_any, matrix_any, faces_any,
    solution_ref, residual_ref,
    start_ref, order_ref, matrix_ref, faces_ref, pairs, wide, held, stars, high, low, rim, total, change, left,
    out_x, out_y, out_xy, in_x, in_y, in_xy, out_z, in_z,
    out_ix, out_iy, out_iz, in_ix, in_iy, in_iz,
    load_sem, send_sem, recv_sem,
):
    gx, gy, gz = lax.axis_index("gx"), lax.axis_index("gy"), lax.axis_index("gz")
    count_x, count_y, count_z = lax.axis_size("gx"), lax.axis_size("gy"), lax.axis_size("gz")
    up_x, down_x = lax.rem(gx + 1, count_x), lax.rem(gx + count_x - 1, count_x)
    first_y, last_y = gy == 0, gy == count_y - 1
    first_z, last_z = gz == 0, gz == count_z - 1
    not_first_y, not_last_y = gy > 0, gy < count_y - 1
    not_first_z, not_last_z = gz > 0, gz < count_z - 1

    barrier = pltpu.get_barrier_semaphore()

    def greet(device):
        pl.semaphore_signal(barrier, inc=1, device_id=device, device_id_type=MESH)

    greet((up_x, gy, gz))
    greet((down_x, gy, gz))

    @pl.when(not_last_y)
    def _():
        greet((gx, gy + 1, gz))
        greet((up_x, gy + 1, gz))

    @pl.when(not_first_y)
    def _():
        greet((gx, gy - 1, gz))
        greet((down_x, gy - 1, gz))

    @pl.when(not_last_z)
    def _():
        greet((gx, gy, gz + 1))

    @pl.when(not_first_z)
    def _():
        greet((gx, gy, gz - 1))

    inverses = inverse_any.reshape(2, 2, 2 * PATCH, PATCH)
    loads = [pltpu.make_async_copy(start_any, start_ref, load_sem.at[0])]
    for x in range(2):
        for y in range(2):
            loads.append(pltpu.make_async_copy(inverses.at[x, y], pairs.at[x, y], load_sem.at[1 + 2 * x + y]))
    loads.append(pltpu.make_async_copy(order_any, order_ref, load_sem.at[5]))
    loads.append(pltpu.make_async_copy(matrix_any, matrix_ref, load_sem.at[6]))
    loads.append(pltpu.make_async_copy(faces_any, faces_ref, load_sem.at[7]))
    for load in loads:
        load.start()

    def blank(x, y, layers, rows):
        for s in range(SWEEPS):
            for l in layers:
                rim[s, x, y, l, rows] = jnp.zeros((rows.stop - rows.start, 128), BF16)

    for x in (1, 2):
        for y in (1, 2):
            blank(x, y, (2,), slice(0, 16))

    @pl.when(first_y)
    def _():
        for x in range(3):
            blank(x, 0, (0, 1, 2), slice(0, 96))

    @pl.when(first_z)
    def _():
        for x in (1, 2):
            for y in (1, 2):
                blank(x, y, (0,), slice(16, 96))

    always = None
    routes = {}

    def route(s, number, src, dst, device, sends, receives):
        copy = pltpu.make_async_remote_copy(
            src_ref=src, dst_ref=dst, send_sem=send_sem.at[s, number], recv_sem=recv_sem.at[s, number],
            device_id=device, device_id_type=MESH,
        )
        routes[s, number] = (copy, sends, receives)

    upper_y, lower_y = gy + 1, gy - 1
    for s in range(SWEEPS):
        here = rim.at[s]
        parts = (
            (Z_FIRST, slice(2, 3), slice(1, 3), slice(16, 96)),
            (Z_SECOND, slice(1, 2), slice(2, 3), slice(16, 96)),
            (Z_HALO, slice(1, 2), slice(1, 2), slice(16, 96)),
        )
        if s > 0:
            parts = (
                (Z_UPPER, slice(2, 3), slice(1, 3), slice(16, 80)),
                (Z_LOWER, slice(1, 2), slice(1, 3), slice(16, 64)),
                (Z_FACE, slice(1, 3), slice(2, 3), slice(80, 96)),
                (Z_LAST_X, slice(1, 2), slice(1, 3), slice(64, 80)),
                (Z_LAST_Y, slice(1, 3), slice(1, 2), slice(80, 96)),
            )
        for number, x, y, rows in parts:
            route(s, number, here.at[x, y, 2, rows], here.at[x, y, 0, rows], (gx, gy, gz + 1),
                  not_last_z, not_first_z)
        for x, y, xy, layers in ((EARLY_X, EARLY_Y, EARLY_XY, slice(1, 3)), (LATE_X, LATE_Y, LATE_XY, slice(0, 1))):
            route(s, x, here.at[2, 1:3, layers], here.at[0, 1:3, layers], (up_x, gy, gz), always, always)
            route(s, y, here.at[1:3, 2, layers], here.at[1:3, 0, layers], (gx, upper_y, gz), not_last_y, not_first_y)
            route(s, xy, here.at[2, 2, layers], here.at[0, 0, layers], (up_x, upper_y, gz), not_last_y, not_first_y)
        for x, y, xy, layers in ((BACK_X, BACK_Y, BACK_XY, slice(0, 1)), (BACK2_X, BACK2_Y, BACK2_XY, slice(1, 3))):
            route(s, x, out_x.at[s, layers], in_x.at[s, layers], (down_x, gy, gz), always, always)
            route(s, y, out_y.at[s, layers], in_y.at[s, layers], (gx, lower_y, gz), not_first_y, not_last_y)
            route(s, xy, out_xy.at[s, layers], in_xy.at[s, layers], (down_x, lower_y, gz), not_first_y, not_last_y)
        for number, rows in (
            (BACK_Z_FIRST, slice(0, 96)),
            (BACK_Z_Y, slice(96, 208)),
            (BACK_Z_X, slice(208, 320)),
            (BACK_Z, slice(320, 448)),
        ):
            route(s, number, out_z.at[s, rows], in_z.at[s, rows], (gx, gy, gz - 1), not_first_z, not_last_z)
        for l in (0, 1):
            route(s, IMAGE_X + l, out_ix.at[s, l], in_ix.at[s, l], (up_x, gy, gz), always, always)
            route(s, IMAGE_Y + l, out_iy.at[s, l], in_iy.at[s, l], (gx, upper_y, gz), not_last_y, not_first_y)
        route(s, IMAGE_Z, out_iz.at[s], in_iz.at[s], (gx, gy, gz + 1), not_last_z, not_first_z)

    def if_(flag, action):
        if flag is None:
            action()
        else:
            pl.when(flag)(action)

    def send(s, *numbers):
        for number in numbers:
            copy, sends, _ = routes[s, number]
            if_(sends, copy.start)

    def receive(s, number, use=None):
        copy, _, receives = routes[s, number]

        def action():
            copy.wait_recv()
            if use is not None:
                use()

        if_(receives, action)

    def clear_left():
        @pl.when(first_y)
        def _():
            left[:, 0, :, 80:96] = jnp.zeros((2, 3, 16, 128), F32)

        @pl.when(first_z)
        def _():
            left[:, :, 0, 0:16] = jnp.zeros((2, 2, 16, 128), F32)

    left[...] = jnp.zeros_like(left)
    loads[0].wait()
    for x in range(2):
        for y in range(2):
            for z in range(2):
                left[x, y, z + 1, 16:79] = start_ref[x, y, 0:63, z, :]
                left[x, y, z + 1, 80:89] = start_ref[x, y, 63:72, z, :]
                left[x, y, z, 0:9] = start_ref[x, y, 72:81, z, :]
    clear_left()

    def round_own(s, l):
        rows = slice(0, 96) if l == 1 else slice(16, 96)
        for x in range(2):
            for y in range(2):
                rim[s, x + 1, y + 1, l, rows] = left[x, y, l, rows].astype(BF16)

    def round_late(s):
        for x in range(2):
            for y in range(2):
                rim[s, x + 1, y + 1, 0, 0:16] = left[x, y, 0, 0:16].astype(BF16)

    def round_faces(s):
        for k in range(2):
            rim[s, 1, k + 1, 2, 64:80] = left[0, k, 2, 64:80].astype(BF16)
            rim[s, k + 1, 1, 2, 80:96] = left[k, 0, 2, 80:96].astype(BF16)

    round_own(0, 1)
    round_own(0, 2)
    round_late(0)

    met = 2 + 2 * not_last_y.astype(jnp.int32) + 2 * not_first_y.astype(jnp.int32)
    met = met + not_last_z.astype(jnp.int32) + not_first_z.astype(jnp.int32)
    pl.semaphore_wait(barrier, met)

    send(0, Z_FIRST, Z_SECOND, Z_HALO)

    def blank_total(s):
        def one(i, carry):
            total[s, i // 12, (i // 3) % 4, i % 3] = jnp.zeros((BLOCK, 128), F32)
            return carry

        lax.fori_loop(0, 48, one, 0)

    def blank_change(s):
        def one(i, carry):
            change[s, i // 12, (i // 3) % 4, i % 3] = jnp.zeros((BLOCK, 128), F32)
            return carry

        lax.fori_loop(0, 48, one, 0)

    dims_nt = (((1,), (1,)), ((), ()))

    lane = lax.broadcasted_iota(jnp.int32, (1, LOCAL), 1)
    face = sum((lane >= INNER + FACE * f).astype(jnp.int32) for f in range(1, 6))
    slot = lane - INNER - FACE * face
    spread = (lax.broadcasted_iota(jnp.int32, (FACE, LOCAL), 0) == slot).astype(F32)
    own_face = (lax.broadcasted_iota(jnp.int32, (6, LOCAL), 0) == face) & (lane >= INNER)
    base = jnp.where(lane < INNER, 16 + lane, 0)
    for f, offset in enumerate((70, 118, 80, 128, 96, 0)):
        base = base + jnp.where((lane >= INNER) & (face == f), offset, 0)
    base = base.astype(F32)
    wide_rows = lax.broadcasted_iota(jnp.int32, (WIDE, LOCAL), 0).astype(F32)

    def element(i, z):
        x, y = i // 2, i % 2
        listed = jnp.dot(faces_ref[x, y, :, z, :].astype(F32).astype(BF16), spread.astype(BF16), preferred_element_type=F32)
        place = base + jnp.sum(jnp.where(own_face, listed, 0.0), axis=0, keepdims=True)
        pick = jnp.where(wide_rows == place, 1.0, 0.0).astype(BF16)
        matrix = matrix_ref[x, y, :, z, :]
        upper = matrix.astype(BF16)
        lower = (matrix - upper.astype(F32)).astype(BF16)
        for part, ref in ((upper, high), (lower, low)):
            rows = jnp.dot(pick, part, preferred_element_type=F32).astype(BF16)
            ref[z, i] = lax.dot_general(rows, pick, dims_nt, preferred_element_type=F32).astype(BF16)

    def elements(i, carry):
        element(i, 0)
        element(i, 1)
        return carry


    star_iota = lax.broadcasted_iota(jnp.int32, (STAR, PATCH), 0)

    def prepare(c, first, last):
        def vertex(i, carry):
            x, y = i // 2, i % 2
            place = star_rows(order_ref[x, y, c : c + 1, :])
            pick = jnp.where(star_iota == place, 1.0, 0.0).astype(BF16)
            rows = jnp.dot(pick, held[x, y, c], preferred_element_type=F32).astype(BF16)
            stars[c, i] = lax.dot_general(rows, pick, dims_nt, preferred_element_type=F32).astype(BF16)
            return carry

        lax.fori_loop(first, last, vertex, 0)

    def star(s, c, x, y):
        pieces = []
        for p in (0, 1):
            for q in (0, 1):
                pieces.append(rim[s, x + p, y + q, c, 16:80])
        for p in (0, 1):
            pieces.append(rim[s, x + p, y + 1, c, 80:96])
        for p in (0, 1):
            for q in (0, 1):
                pieces.append(rim[s, x + p, y + q, c, 0:16])
        for p in (0, 1):
            for q in (0, 1):
                pieces.append(rim[s, x + p, y + q, c + 1, 16:80])
        for p in (0, 1):
            pieces.append(rim[s, x + p, y + 1, c + 1, 80:96])
        return jnp.concatenate(pieces, axis=0)

    def solve(s, c, upper):
        first, last = (LOWER, STAR) if upper else (0, LOWER)
        solved = {}
        for x in (0, 1):
            for y in (0, 1):
                solved[x, y] = jnp.dot(stars[c, 2 * x + y, first:last], star(s, c, x, y), preferred_element_type=F32)
        l = c + 1 if upper else c
        for x in range(3):
            for y in range(3):
                near = [(x - p, y - q, p, q) for p in (0, 1) for q in (0, 1) if 0 <= x - p < 2 and 0 <= y - q < 2]
                cell = [solved[i, j][64 * (2 * p + q) : 64 * (2 * p + q) + 64] for i, j, p, q in near]
                total[s, x, y, l, 16:80] += functools.reduce(jnp.add, cell)
                side = [solved[i, j][256 + 16 * p : 272 + 16 * p] for i, j, p, q in near if q == 1]
                if side:
                    total[s, x, y, l, 80:96] += functools.reduce(jnp.add, side)
                if not upper:
                    base = [solved[i, j][288 + 16 * (2 * p + q) : 304 + 16 * (2 * p + q)] for i, j, p, q in near]
                    total[s, x, y, l, 0:16] += functools.reduce(jnp.add, base)

    def send_back(s, layers, numbers):
        for l in layers:
            for k in (1, 2):
                out_x[s, l, k - 1, 0:96] = total[s, 0, k, l].astype(BF16)
                out_x[s, l, k - 1, 96:112] = total[s, 1, k, l, 64:80].astype(BF16)
        send(s, numbers[0])
        for l in layers:
            for k in (1, 2):
                out_y[s, l, k - 1, 0:96] = total[s, k, 0, l].astype(BF16)
                out_y[s, l, k - 1, 96:112] = total[s, k, 1, l, 80:96].astype(BF16)
        send(s, numbers[1])
        for l in layers:
            out_xy[s, l, 0:96] = total[s, 0, 0, l].astype(BF16)
            out_xy[s, l, 96:112] = total[s, 1, 0, l, 64:80].astype(BF16)
            out_xy[s, l, 112:128] = total[s, 0, 1, l, 80:96].astype(BF16)
        send(s, numbers[2])

    def take_back(s, layers, numbers):
        def from_x():
            for l in layers:
                for k in (1, 2):
                    total[s, 2, k, l] += in_x[s, l, k - 1, 0:96].astype(F32)
                    total[s, 3, k, l, 64:80] += in_x[s, l, k - 1, 96:112].astype(F32)

        def from_y():
            for l in layers:
                for k in (1, 2):
                    total[s, k, 2, l] += in_y[s, l, k - 1, 0:96].astype(F32)
                    total[s, k, 3, l, 80:96] += in_y[s, l, k - 1, 96:112].astype(F32)

        def from_xy():
            for l in layers:
                total[s, 2, 2, l] += in_xy[s, l, 0:96].astype(F32)
                total[s, 3, 2, l, 64:80] += in_xy[s, l, 96:112].astype(F32)
                total[s, 2, 3, l, 80:96] += in_xy[s, l, 112:128].astype(F32)

        for number, use, then in ((numbers[1], from_y, BACK_Z_Y), (numbers[0], from_x, BACK_Z_X), (numbers[2], from_xy, None)):
            receive(s, number, use)
            if then is not None and layers == (0,):
                if then == BACK_Z_Y:
                    out_z[s, 96:192] = total[s, 1, 2, 0].astype(BF16)
                    out_z[s, 192:208] = total[s, 1, 3, 0, 80:96].astype(BF16)
                else:
                    out_z[s, 208:304] = total[s, 2, 1, 0].astype(BF16)
                    out_z[s, 304:320] = total[s, 3, 1, 0, 64:80].astype(BF16)
                send(s, then)

    def send_back_z_first(s):
        out_z[s, 0:BLOCK] = total[s, 1, 1, 0].astype(BF16)
        send(s, BACK_Z_FIRST)

    def send_back_z(s):
        out_z[s, 320:416] = total[s, 2, 2, 0].astype(BF16)
        out_z[s, 416:432] = total[s, 3, 2, 0, 64:80].astype(BF16)
        out_z[s, 432:448] = total[s, 2, 3, 0, 80:96].astype(BF16)
        send(s, BACK_Z)

    def take_back_z(s):
        def first():
            total[s, 1, 1, 2] += in_z[s, 0:96].astype(F32)

        def from_y():
            total[s, 1, 2, 2] += in_z[s, 96:192].astype(F32)
            total[s, 1, 3, 2, 80:96] += in_z[s, 192:208].astype(F32)

        def from_x():
            total[s, 2, 1, 2] += in_z[s, 208:304].astype(F32)
            total[s, 3, 1, 2, 64:80] += in_z[s, 304:320].astype(F32)

        def last():
            total[s, 2, 2, 2] += in_z[s, 320:416].astype(F32)
            total[s, 3, 2, 2, 64:80] += in_z[s, 416:432].astype(F32)
            total[s, 2, 3, 2, 80:96] += in_z[s, 432:448].astype(F32)

        receive(s, BACK_Z_FIRST, first)
        receive(s, BACK_Z_Y, from_y)
        receive(s, BACK_Z_X, from_x)
        receive(s, BACK_Z, last)

    def clear_total(s):
        @pl.when(first_y)
        def _():
            total[s, 1:3, 1, :, 80:96] = jnp.zeros((2, 3, 16, 128), F32)

        @pl.when(first_z)
        def _():
            total[s, 1:3, 1:3, 0, 0:16] = jnp.zeros((2, 2, 16, 128), F32)

    def images(s, l):
        for x in (1, 2):
            for y in (1, 2):
                i = 2 * x + y - 3
                local = jnp.concatenate(
                    [
                        total[s, x, y, l],
                        total[s, x, y, l - 1, 0:16],
                        total[s, x + 1, y, l, 64:80],
                        total[s, x, y + 1, l, 80:96],
                    ],
                    axis=0,
                )
                upper = local.astype(BF16)
                lower = (local - upper.astype(F32)).astype(BF16)
                image = jnp.dot(high[l - 1, i], upper, preferred_element_type=F32)
                image += jnp.dot(high[l - 1, i], lower, preferred_element_type=F32)
                image += jnp.dot(low[l - 1, i], upper, preferred_element_type=F32)
                change[s, x, y, l] += image[0:96]
                change[s, x, y, l - 1, 0:16] += image[96:112]
                change[s, x + 1, y, l, 64:80] += image[112:128]
                change[s, x, y + 1, l, 80:96] += image[128:144]

    def send_images(s, l):
        for k in (1, 2):
            m = 16 * (k - 1)
            out_ix[s, l - 1, m : m + 16] = change[s, 3, k, l, 64:80].astype(BF16)
            out_iy[s, l - 1, m : m + 16] = change[s, k, 3, l, 80:96].astype(BF16)
        send(s, IMAGE_X + l - 1, IMAGE_Y + l - 1)

    def send_images_z(s):
        for x in (1, 2):
            for y in (1, 2):
                m = 16 * (2 * x + y - 3)
                out_iz[s, m : m + 16] = change[s, x, y, 2, 0:16].astype(BF16)
        send(s, IMAGE_Z)

    def take_images(s, l):
        def from_x():
            for k in (0, 1):
                left[0, k, l, 64:80] -= in_ix[s, l - 1, 16 * k : 16 * k + 16].astype(F32)

        def from_y():
            for k in (0, 1):
                left[k, 0, l, 80:96] -= in_iy[s, l - 1, 16 * k : 16 * k + 16].astype(F32)

        receive(s, IMAGE_X + l - 1, from_x)
        receive(s, IMAGE_Y + l - 1, from_y)

    def take_images_z(s):
        def use():
            for x in (1, 2):
                for y in (1, 2):
                    m = 16 * (2 * x + y - 3)
                    change[s, x, y, 0, 0:16] += in_iz[s, m : m + 16].astype(F32)

        receive(s, IMAGE_Z, use)

    def update_own(s, l):
        rows = slice(0, 96) if l == 1 else slice(16, 96)
        for x in (1, 2):
            for y in (1, 2):
                left[x - 1, y - 1, l, rows] -= change[s, x, y, l, rows]
        clear_left()

    def update_late(s):
        for x in (1, 2):
            for y in (1, 2):
                left[x - 1, y - 1, 0, 0:16] -= change[s, x, y, 0, 0:16]
        clear_left()

    def write_early():
        for x in range(2):
            for y in range(2):
                for z in range(2):
                    block = total[0, x + 1, y + 1, z + 1] + total[1, x + 1, y + 1, z + 1]
                    solution_ref[x, y, 0:63, z, :] = block[16:79]
                    solution_ref[x, y, 63:72, z, :] = block[80:89]
                    lower = total[0, x + 1, y + 1, z, 0:16] + total[1, x + 1, y + 1, z, 0:16]
                    solution_ref[x, y, 72:81, z, :] = lower[0:9]
                    residual_ref[x, y, 0:63, z, :] = left[x, y, z + 1, 16:79]
                    residual_ref[x, y, 63:72, z, :] = left[x, y, z + 1, 80:89]
                residual_ref[x, y, 72:81, 1, :] = left[x, y, 1, 0:9]

    early = (EARLY_X, EARLY_Y, EARLY_XY)
    late = (LATE_X, LATE_Y, LATE_XY)
    back = (BACK_X, BACK_Y, BACK_XY)
    back2 = (BACK2_X, BACK2_Y, BACK2_XY)
    z_early = (Z_UPPER, Z_LOWER, Z_FACE)
    z_late = (Z_LAST_X, Z_LAST_Y)

    blank_total(0)
    for load in loads[1:]:
        load.wait()

    def separate(i, carry):
        x, y = i // 2, i % 2
        for k in range(5):
            width = min(128, PATCH - 128 * k)
            wide[k, :, 0:width] = pairs[x, y, :, 128 * k : 128 * k + width].astype(F32)
        for z in range(2):
            for k in range(5):
                width = min(128, PATCH - 128 * k)
                rows = wide[k, pl.ds(z, PATCH, stride=2), :].astype(BF16)
                held[x, y, z, :, 128 * k : 128 * k + width] = rows[:, 0:width]
        return carry

    lax.fori_loop(0, 4, separate, 0)
    send(0, *early)
    prepare(0, 0, 3)
    for s in range(SWEEPS):
        if s == 0:
            receive(s, Z_FIRST)
            send(s, LATE_X, LATE_XY)
            receive(s, Z_SECOND)
            send(s, LATE_Y)
            prepare(0, 3, 4)
            receive(s, Z_HALO)
            prepare(1, 0, 1)
            for number in early:
                receive(s, number)
        else:
            take_images_z(s - 1)
            update_late(s - 1)
            round_late(s)
            for number in z_early + z_late:
                receive(s, number)
            send(s, *late)
            for number in early:
                receive(s, number)
            solve(s, 1, False)
            solve(s, 1, True)
        for number in late:
            receive(s, number)
        solve(s, 0, False)
        send_back_z_first(s)
        send_back(s, (0,), back)
        solve(s, 0, True)
        if s == 0:
            prepare(1, 1, 3)
        else:
            send_back(s, (1, 2), back2)
        take_back(s, (0,), back)
        send_back_z(s)
        if s == 0:
            prepare(1, 3, 4)
            solve(s, 1, False)
            solve(s, 1, True)
            send_back(s, (1, 2), back2)
            lax.fori_loop(0, 4, elements, 0)
            blank_change(0)
        take_back(s, (1, 2), back2)
        if s < SWEEPS - 1:
            take_back_z(s)
            clear_total(s)
            images(s, 2)
            send_images(s, 2)
            update_own(s, 2)
            round_own(s + 1, 2)
            send(s + 1, *z_early)
            send_images_z(s)
            images(s, 1)
            send_images(s, 1)
            update_own(s, 1)
            take_images(s, 2)
            round_faces(s + 1)
            send(s + 1, *z_late)
            blank_total(s + 1)
            take_images(s, 1)
            round_own(s + 1, 1)
            send(s + 1, *early)
            blank_change(s + 1)
        else:
            clear_total(s)
            images(s, 1)
            send_images(s, 1)
            take_back_z(s)
            clear_total(s)
            images(s, 2)
            send_images_z(s)
            send_images(s, 2)
            update_own(s, 1)
            update_own(s, 2)
            write_early()
            take_images(s, 1)
            take_images(s, 2)

    for z in range(2):
        for k in range(2):
            residual_ref[0, k, 54:63, z, :] = left[0, k, z + 1, 70:79]
            residual_ref[k, 0, 63:72, z, :] = left[k, 0, z + 1, 80:89]
    take_images_z(SWEEPS - 1)
    update_late(SWEEPS - 1)
    for x in range(2):
        for y in range(2):
            residual_ref[x, y, 72:81, 0, :] = left[x, y, 0, 0:9]

    for copy, sends, _ in routes.values():
        if_(sends, copy.wait_send)


def body(residual_start, patch_inverse, patch_order, element_matrix, face_order):
    swapped = lambda value: jnp.transpose(value, (0, 1, 3, 2, 4))
    residual_start = swapped(residual_start)
    shape = jax.ShapeDtypeStruct(residual_start.shape, F32)
    vmem = pl.BlockSpec(memory_space=pltpu.VMEM)
    total, left = pl.pallas_call(
        kernel,
        out_shape=(shape, shape),
        in_specs=[pl.BlockSpec(memory_space=pltpu.HBM)] * 5,
        out_specs=(vmem, vmem),
        scratch_shapes=[
            pltpu.VMEM(residual_start.shape, F32),
            pltpu.VMEM(patch_order.shape, jnp.int32),
            pltpu.VMEM((2, 2, LOCAL, 2, LOCAL), F32),
            pltpu.VMEM((2, 2, 6, 2, FACE), jnp.int32),
            pltpu.VMEM((2, 2, 2 * PATCH, PATCH), BF16),
            pltpu.VMEM((5, 2 * PATCH, 128), F32),
            pltpu.VMEM((2, 2, 2, PATCH, PATCH), BF16),
            pltpu.VMEM((2, 4, STAR, STAR), BF16),
            pltpu.VMEM((2, 4, WIDE, WIDE), BF16),
            pltpu.VMEM((2, 4, WIDE, WIDE), BF16),
            pltpu.VMEM((SWEEPS, 3, 3, 3, BLOCK, 128), BF16),
            pltpu.VMEM((SWEEPS, 4, 4, 3, BLOCK, 128), F32),
            pltpu.VMEM((SWEEPS, 4, 4, 3, BLOCK, 128), F32),
            pltpu.VMEM((2, 2, 3, BLOCK, 128), F32),
            pltpu.VMEM((SWEEPS, 3, 2, 112, 128), BF16),
            pltpu.VMEM((SWEEPS, 3, 2, 112, 128), BF16),
            pltpu.VMEM((SWEEPS, 3, 128, 128), BF16),
            pltpu.VMEM((SWEEPS, 3, 2, 112, 128), BF16),
            pltpu.VMEM((SWEEPS, 3, 2, 112, 128), BF16),
            pltpu.VMEM((SWEEPS, 3, 128, 128), BF16),
            pltpu.VMEM((SWEEPS, 448, 128), BF16),
            pltpu.VMEM((SWEEPS, 448, 128), BF16),
            pltpu.VMEM((SWEEPS, 2, 32, 128), BF16),
            pltpu.VMEM((SWEEPS, 2, 32, 128), BF16),
            pltpu.VMEM((SWEEPS, 64, 128), BF16),
            pltpu.VMEM((SWEEPS, 2, 32, 128), BF16),
            pltpu.VMEM((SWEEPS, 2, 32, 128), BF16),
            pltpu.VMEM((SWEEPS, 64, 128), BF16),
            pltpu.SemaphoreType.DMA((8,)),
            pltpu.SemaphoreType.DMA((SWEEPS, COPIES)),
            pltpu.SemaphoreType.DMA((SWEEPS, COPIES)),
        ],
        compiler_params=pltpu.CompilerParams(
            collective_id=0, has_side_effects=True, vmem_limit_bytes=60 * 1024 * 1024
        ),
    )(residual_start, swapped(patch_inverse), patch_order, swapped(element_matrix), swapped(face_order))

    def finish(first, second, first_out, second_out, sem):
        copies = [
            pltpu.make_async_copy(first, first_out, sem.at[0]),
            pltpu.make_async_copy(second, second_out, sem.at[1]),
        ]
        for copy in copies:
            copy.start()
        for copy in copies:
            copy.wait()

    total, left = pl.pallas_call(
        finish,
        out_shape=(shape, shape),
        in_specs=[vmem, vmem],
        out_specs=(pl.BlockSpec(memory_space=pltpu.HBM), pl.BlockSpec(memory_space=pltpu.HBM)),
        scratch_shapes=[pltpu.SemaphoreType.DMA((2,))],
    )(total, left)
    return swapped(total), swapped(left)


def solution(mesh):
    return jax.shard_map(
        body,
        mesh=mesh,
        in_specs=(
            P("gx", "gy", "gz", None, None),
            P("gx", "gy", "gz", None, None),
            P("gx", "gy", "gz", None),
            P("gx", "gy", "gz", None, None),
            P("gx", "gy", "gz", None, None),
        ),
        out_specs=(P("gx", "gy", "gz", None, None), P("gx", "gy", "gz", None, None)),
        check_vma=False,
    )
```

```python
import functools

import jax
import jax.numpy as jnp
from jax import lax
from jax.experimental import pallas as pl
from jax.experimental.pallas import tpu as pltpu
from jax.sharding import PartitionSpec as P

INNER = 54
FACE = 9
SWEEPS = 2
PATCH = 540
LOCAL = 108
STAR = 640
WIDE = 144
BLOCK = 96
MESH = pl.DeviceIdType.MESH
F32 = jnp.float32
BF16 = jnp.bfloat16

Z_HALO = 0
EARLY_X, EARLY_Y, EARLY_XY = 1, 2, 3
LATE_X, LATE_Y, LATE_XY = 4, 5, 6
BACK_X, BACK_Y, BACK_XY = 7, 8, 9
BACK2_X, BACK2_Y, BACK2_XY = 10, 11, 12
BACK_Z = 13
IMAGE_X, IMAGE_Y = 14, 16
IMAGE_Z = 18
Z_UPPER, Z_LOWER, Z_FACE, Z_LAST_X, Z_LAST_Y = 19, 20, 21, 22, 23
BACK_Z_FIRST, BACK_Z_Y, BACK_Z_X = 24, 25, 26
Z_FIRST, Z_SECOND = 27, 28
COPIES = 29

CELL_ROWS = [64 * (m // 2) + 352 * (m % 2) for m in range(8)]
Y_ROWS = [256 + 16 * (g // 2) + (608 - 256) * (g % 2) for g in range(4)]
Z_ROWS = [288 + 16 * h for h in range(4)]
LOWER = 352
SEGMENTS = (
    [(INNER * m, CELL_ROWS[m]) for m in range(8)]
    + [(8 * INNER + FACE * f, CELL_ROWS[4 + f] + INNER) for f in range(4)]
    + [(8 * INNER + FACE * (4 + g), Y_ROWS[g]) for g in range(4)]
    + [(8 * INNER + FACE * (8 + h), Z_ROWS[h]) for h in range(4)]
)


def star_rows(order):
    place, shift = order, 0
    for first, row in SEGMENTS:
        step = row - first - shift
        shift += step
        if step:
            place = place + step * (order >= first).astype(jnp.int32)
    return place


def kernel(
    start_any, inverse_any, order_any, matrix_any, faces_any,
    solution_ref, residual_ref,
    start_ref, order_ref, matrix_ref, faces_ref, pairs, wide, held, stars, high, low, rim, total, change, left,
    out_x, out_y, out_xy, in_x, in_y, in_xy, out_z, in_z,
    out_ix, out_iy, out_iz, in_ix, in_iy, in_iz,
    load_sem, send_sem, recv_sem,
):
    gx, gy, gz = lax.axis_index("gx"), lax.axis_index("gy"), lax.axis_index("gz")
    count_x, count_y, count_z = lax.axis_size("gx"), lax.axis_size("gy"), lax.axis_size("gz")
    up_x, down_x = lax.rem(gx + 1, count_x), lax.rem(gx + count_x - 1, count_x)
    first_y, last_y = gy == 0, gy == count_y - 1
    first_z, last_z = gz == 0, gz == count_z - 1
    not_first_y, not_last_y = gy > 0, gy < count_y - 1
    not_first_z, not_last_z = gz > 0, gz < count_z - 1

    barrier = pltpu.get_barrier_semaphore()

    def greet(device):
        pl.semaphore_signal(barrier, inc=1, device_id=device, device_id_type=MESH)

    greet((up_x, gy, gz))
    greet((down_x, gy, gz))

    @pl.when(not_last_y)
    def _():
        greet((gx, gy + 1, gz))
        greet((up_x, gy + 1, gz))

    @pl.when(not_first_y)
    def _():
        greet((gx, gy - 1, gz))
        greet((down_x, gy - 1, gz))

    @pl.when(not_last_z)
    def _():
        greet((gx, gy, gz + 1))

    @pl.when(not_first_z)
    def _():
        greet((gx, gy, gz - 1))

    inverses = inverse_any.reshape(2, 2, 2 * PATCH, PATCH)
    loads = [pltpu.make_async_copy(start_any, start_ref, load_sem.at[0])]
    for x in range(2):
        for y in range(2):
            loads.append(pltpu.make_async_copy(inverses.at[x, y], pairs.at[x, y], load_sem.at[1 + 2 * x + y]))
    loads.append(pltpu.make_async_copy(order_any, order_ref, load_sem.at[5]))
    loads.append(pltpu.make_async_copy(matrix_any, matrix_ref, load_sem.at[6]))
    loads.append(pltpu.make_async_copy(faces_any, faces_ref, load_sem.at[7]))
    for load in loads:
        load.start()

    def blank(x, y, layers, rows):
        for s in range(SWEEPS):
            for l in layers:
                rim[s, x, y, l, rows] = jnp.zeros((rows.stop - rows.start, 128), BF16)

    for x in (1, 2):
        for y in (1, 2):
            blank(x, y, (2,), slice(0, 16))

    @pl.when(first_y)
    def _():
        for x in range(3):
            blank(x, 0, (0, 1, 2), slice(0, 96))

    @pl.when(first_z)
    def _():
        for x in (1, 2):
            for y in (1, 2):
                blank(x, y, (0,), slice(16, 96))

    always = None
    routes = {}

    def route(s, number, src, dst, device, sends, receives):
        copy = pltpu.make_async_remote_copy(
            src_ref=src, dst_ref=dst, send_sem=send_sem.at[s, number], recv_sem=recv_sem.at[s, number],
            device_id=device, device_id_type=MESH,
        )
        routes[s, number] = (copy, sends, receives)

    upper_y, lower_y = gy + 1, gy - 1
    for s in range(SWEEPS):
        here = rim.at[s]
        parts = (
            (Z_FIRST, slice(2, 3), slice(1, 3), slice(16, 96)),
            (Z_SECOND, slice(1, 2), slice(2, 3), slice(16, 96)),
            (Z_HALO, slice(1, 2), slice(1, 2), slice(16, 96)),
        )
        if s > 0:
            parts = (
                (Z_UPPER, slice(2, 3), slice(1, 3), slice(16, 80)),
                (Z_LOWER, slice(1, 2), slice(1, 3), slice(16, 64)),
                (Z_FACE, slice(1, 3), slice(2, 3), slice(80, 96)),
                (Z_LAST_X, slice(1, 2), slice(1, 3), slice(64, 80)),
                (Z_LAST_Y, slice(1, 3), slice(1, 2), slice(80, 96)),
            )
        for number, x, y, rows in parts:
            route(s, number, here.at[x, y, 2, rows], here.at[x, y, 0, rows], (gx, gy, gz + 1),
                  not_last_z, not_first_z)
        for x, y, xy, layers in ((EARLY_X, EARLY_Y, EARLY_XY, slice(1, 3)), (LATE_X, LATE_Y, LATE_XY, slice(0, 1))):
            route(s, x, here.at[2, 1:3, layers], here.at[0, 1:3, layers], (up_x, gy, gz), always, always)
            route(s, y, here.at[1:3, 2, layers], here.at[1:3, 0, layers], (gx, upper_y, gz), not_last_y, not_first_y)
            route(s, xy, here.at[2, 2, layers], here.at[0, 0, layers], (up_x, upper_y, gz), not_last_y, not_first_y)
        for x, y, xy, layers in ((BACK_X, BACK_Y, BACK_XY, slice(0, 1)), (BACK2_X, BACK2_Y, BACK2_XY, slice(1, 3))):
            route(s, x, out_x.at[s, layers], in_x.at[s, layers], (down_x, gy, gz), always, always)
            route(s, y, out_y.at[s, layers], in_y.at[s, layers], (gx, lower_y, gz), not_first_y, not_last_y)
            route(s, xy, out_xy.at[s, layers], in_xy.at[s, layers], (down_x, lower_y, gz), not_first_y, not_last_y)
        for number, rows in (
            (BACK_Z_FIRST, slice(0, 96)),
            (BACK_Z_Y, slice(96, 208)),
            (BACK_Z_X, slice(208, 320)),
            (BACK_Z, slice(320, 448)),
        ):
            route(s, number, out_z.at[s, rows], in_z.at[s, rows], (gx, gy, gz - 1), not_first_z, not_last_z)
        for l in (0, 1):
            route(s, IMAGE_X + l, out_ix.at[s, l], in_ix.at[s, l], (up_x, gy, gz), always, always)
            route(s, IMAGE_Y + l, out_iy.at[s, l], in_iy.at[s, l], (gx, upper_y, gz), not_last_y, not_first_y)
        route(s, IMAGE_Z, out_iz.at[s], in_iz.at[s], (gx, gy, gz + 1), not_last_z, not_first_z)

    def if_(flag, action):
        if flag is None:
            action()
        else:
            pl.when(flag)(action)

    def send(s, *numbers):
        for number in numbers:
            copy, sends, _ = routes[s, number]
            if_(sends, copy.start)

    def receive(s, number, use=None):
        copy, _, receives = routes[s, number]

        def action():
            copy.wait_recv()
            if use is not None:
                use()

        if_(receives, action)

    def clear_left():
        @pl.when(first_y)
        def _():
            left[:, 0, :, 80:96] = jnp.zeros((2, 3, 16, 128), F32)

        @pl.when(first_z)
        def _():
            left[:, :, 0, 0:16] = jnp.zeros((2, 2, 16, 128), F32)

    left[...] = jnp.zeros_like(left)
    loads[0].wait()
    for x in range(2):
        for y in range(2):
            for z in range(2):
                left[x, y, z + 1, 16:79] = start_ref[x, y, 0:63, z, :]
                left[x, y, z + 1, 80:89] = start_ref[x, y, 63:72, z, :]
                left[x, y, z, 0:9] = start_ref[x, y, 72:81, z, :]
    clear_left()

    def round_own(s, l):
        rows = slice(0, 96) if l == 1 else slice(16, 96)
        for x in range(2):
            for y in range(2):
                rim[s, x + 1, y + 1, l, rows] = left[x, y, l, rows].astype(BF16)

    def round_late(s):
        for x in range(2):
            for y in range(2):
                rim[s, x + 1, y + 1, 0, 0:16] = left[x, y, 0, 0:16].astype(BF16)

    def round_faces(s):
        for k in range(2):
            rim[s, 1, k + 1, 2, 64:80] = left[0, k, 2, 64:80].astype(BF16)
            rim[s, k + 1, 1, 2, 80:96] = left[k, 0, 2, 80:96].astype(BF16)

    round_own(0, 1)
    round_own(0, 2)
    round_late(0)

    met = 2 + 2 * not_last_y.astype(jnp.int32) + 2 * not_first_y.astype(jnp.int32)
    met = met + not_last_z.astype(jnp.int32) + not_first_z.astype(jnp.int32)
    pl.semaphore_wait(barrier, met)

    send(0, Z_FIRST, Z_SECOND, Z_HALO)

    def blank_total(s):
        def one(i, carry):
            total[s, i // 12, (i // 3) % 4, i % 3] = jnp.zeros((BLOCK, 128), F32)
            return carry

        lax.fori_loop(0, 48, one, 0)

    def blank_change(s):
        def one(i, carry):
            change[s, i // 12, (i // 3) % 4, i % 3] = jnp.zeros((BLOCK, 128), F32)
            return carry

        lax.fori_loop(0, 48, one, 0)

    dims_nt = (((1,), (1,)), ((), ()))

    lane = lax.broadcasted_iota(jnp.int32, (1, LOCAL), 1)
    face = sum((lane >= INNER + FACE * f).astype(jnp.int32) for f in range(1, 6))
    slot = lane - INNER - FACE * face
    spread = (lax.broadcasted_iota(jnp.int32, (FACE, LOCAL), 0) == slot).astype(F32)
    own_face = (lax.broadcasted_iota(jnp.int32, (6, LOCAL), 0) == face) & (lane >= INNER)
    base = jnp.where(lane < INNER, 16 + lane, 0)
    for f, offset in enumerate((70, 118, 80, 128, 96, 0)):
        base = base + jnp.where((lane >= INNER) & (face == f), offset, 0)
    base = base.astype(F32)
    wide_rows = lax.broadcasted_iota(jnp.int32, (WIDE, LOCAL), 0).astype(F32)

    def element(i, z):
        x, y = i // 2, i % 2
        listed = jnp.dot(faces_ref[x, y, :, z, :].astype(F32).astype(BF16), spread.astype(BF16), preferred_element_type=F32)
        place = base + jnp.sum(jnp.where(own_face, listed, 0.0), axis=0, keepdims=True)
        pick = jnp.where(wide_rows == place, 1.0, 0.0).astype(BF16)
        matrix = matrix_ref[x, y, :, z, :]
        upper = matrix.astype(BF16)
        lower = (matrix - upper.astype(F32)).astype(BF16)
        for part, ref in ((upper, high), (lower, low)):
            rows = jnp.dot(pick, part, preferred_element_type=F32).astype(BF16)
            ref[z, i] = lax.dot_general(rows, pick, dims_nt, preferred_element_type=F32).astype(BF16)

    def elements(i, carry):
        element(i, 0)
        element(i, 1)
        return carry


    star_iota = lax.broadcasted_iota(jnp.int32, (STAR, PATCH), 0)

    def prepare(c, first, last):
        def vertex(i, carry):
            x, y = i // 2, i % 2
            place = star_rows(order_ref[x, y, c : c + 1, :])
            pick = jnp.where(star_iota == place, 1.0, 0.0).astype(BF16)
            rows = jnp.dot(pick, held[x, y, c], preferred_element_type=F32).astype(BF16)
            stars[c, i] = lax.dot_general(rows, pick, dims_nt, preferred_element_type=F32).astype(BF16)
            return carry

        lax.fori_loop(first, last, vertex, 0, unroll=True)

    def star(s, c, x, y):
        pieces = []
        for p in (0, 1):
            for q in (0, 1):
                pieces.append(rim[s, x + p, y + q, c, 16:80])
        for p in (0, 1):
            pieces.append(rim[s, x + p, y + 1, c, 80:96])
        for p in (0, 1):
            for q in (0, 1):
                pieces.append(rim[s, x + p, y + q, c, 0:16])
        for p in (0, 1):
            for q in (0, 1):
                pieces.append(rim[s, x + p, y + q, c + 1, 16:80])
        for p in (0, 1):
            pieces.append(rim[s, x + p, y + 1, c + 1, 80:96])
        return jnp.concatenate(pieces, axis=0)

    def solve(s, c, upper):
        first, last = (LOWER, STAR) if upper else (0, LOWER)
        solved = {}
        for x in (0, 1):
            for y in (0, 1):
                solved[x, y] = jnp.dot(stars[c, 2 * x + y, first:last], star(s, c, x, y), preferred_element_type=F32)
        l = c + 1 if upper else c
        for x in range(3):
            for y in range(3):
                near = [(x - p, y - q, p, q) for p in (0, 1) for q in (0, 1) if 0 <= x - p < 2 and 0 <= y - q < 2]
                cell = [solved[i, j][64 * (2 * p + q) : 64 * (2 * p + q) + 64] for i, j, p, q in near]
                total[s, x, y, l, 16:80] += functools.reduce(jnp.add, cell)
                side = [solved[i, j][256 + 16 * p : 272 + 16 * p] for i, j, p, q in near if q == 1]
                if side:
                    total[s, x, y, l, 80:96] += functools.reduce(jnp.add, side)
                if not upper:
                    base = [solved[i, j][288 + 16 * (2 * p + q) : 304 + 16 * (2 * p + q)] for i, j, p, q in near]
                    total[s, x, y, l, 0:16] += functools.reduce(jnp.add, base)

    def send_back(s, layers, numbers):
        for l in layers:
            for k in (1, 2):
                out_x[s, l, k - 1, 0:96] = total[s, 0, k, l].astype(BF16)
                out_x[s, l, k - 1, 96:112] = total[s, 1, k, l, 64:80].astype(BF16)
        send(s, numbers[0])
        for l in layers:
            for k in (1, 2):
                out_y[s, l, k - 1, 0:96] = total[s, k, 0, l].astype(BF16)
                out_y[s, l, k - 1, 96:112] = total[s, k, 1, l, 80:96].astype(BF16)
        send(s, numbers[1])
        for l in layers:
            out_xy[s, l, 0:96] = total[s, 0, 0, l].astype(BF16)
            out_xy[s, l, 96:112] = total[s, 1, 0, l, 64:80].astype(BF16)
            out_xy[s, l, 112:128] = total[s, 0, 1, l, 80:96].astype(BF16)
        send(s, numbers[2])

    def take_back(s, layers, numbers):
        def from_x():
            for l in layers:
                for k in (1, 2):
                    total[s, 2, k, l] += in_x[s, l, k - 1, 0:96].astype(F32)
                    total[s, 3, k, l, 64:80] += in_x[s, l, k - 1, 96:112].astype(F32)

        def from_y():
            for l in layers:
                for k in (1, 2):
                    total[s, k, 2, l] += in_y[s, l, k - 1, 0:96].astype(F32)
                    total[s, k, 3, l, 80:96] += in_y[s, l, k - 1, 96:112].astype(F32)

        def from_xy():
            for l in layers:
                total[s, 2, 2, l] += in_xy[s, l, 0:96].astype(F32)
                total[s, 3, 2, l, 64:80] += in_xy[s, l, 96:112].astype(F32)
                total[s, 2, 3, l, 80:96] += in_xy[s, l, 112:128].astype(F32)

        for number, use, then in ((numbers[1], from_y, BACK_Z_Y), (numbers[0], from_x, BACK_Z_X), (numbers[2], from_xy, None)):
            receive(s, number, use)
            if then is not None and layers == (0,):
                if then == BACK_Z_Y:
                    out_z[s, 96:192] = total[s, 1, 2, 0].astype(BF16)
                    out_z[s, 192:208] = total[s, 1, 3, 0, 80:96].astype(BF16)
                else:
                    out_z[s, 208:304] = total[s, 2, 1, 0].astype(BF16)
                    out_z[s, 304:320] = total[s, 3, 1, 0, 64:80].astype(BF16)
                send(s, then)

    def send_back_z_first(s):
        out_z[s, 0:BLOCK] = total[s, 1, 1, 0].astype(BF16)
        send(s, BACK_Z_FIRST)

    def send_back_z(s):
        out_z[s, 320:416] = total[s, 2, 2, 0].astype(BF16)
        out_z[s, 416:432] = total[s, 3, 2, 0, 64:80].astype(BF16)
        out_z[s, 432:448] = total[s, 2, 3, 0, 80:96].astype(BF16)
        send(s, BACK_Z)

    def take_back_z(s):
        def first():
            total[s, 1, 1, 2] += in_z[s, 0:96].astype(F32)

        def from_y():
            total[s, 1, 2, 2] += in_z[s, 96:192].astype(F32)
            total[s, 1, 3, 2, 80:96] += in_z[s, 192:208].astype(F32)

        def from_x():
            total[s, 2, 1, 2] += in_z[s, 208:304].astype(F32)
            total[s, 3, 1, 2, 64:80] += in_z[s, 304:320].astype(F32)

        def last():
            total[s, 2, 2, 2] += in_z[s, 320:416].astype(F32)
            total[s, 3, 2, 2, 64:80] += in_z[s, 416:432].astype(F32)
            total[s, 2, 3, 2, 80:96] += in_z[s, 432:448].astype(F32)

        receive(s, BACK_Z_FIRST, first)
        receive(s, BACK_Z_Y, from_y)
        receive(s, BACK_Z_X, from_x)
        receive(s, BACK_Z, last)

    def clear_total(s):
        @pl.when(first_y)
        def _():
            total[s, 1:3, 1, :, 80:96] = jnp.zeros((2, 3, 16, 128), F32)

        @pl.when(first_z)
        def _():
            total[s, 1:3, 1:3, 0, 0:16] = jnp.zeros((2, 2, 16, 128), F32)

    def images(s, l):
        for x in (1, 2):
            for y in (1, 2):
                i = 2 * x + y - 3
                local = jnp.concatenate(
                    [
                        total[s, x, y, l],
                        total[s, x, y, l - 1, 0:16],
                        total[s, x + 1, y, l, 64:80],
                        total[s, x, y + 1, l, 80:96],
                    ],
                    axis=0,
                )
                upper = local.astype(BF16)
                lower = (local - upper.astype(F32)).astype(BF16)
                image = jnp.dot(high[l - 1, i], upper, preferred_element_type=F32)
                image += jnp.dot(high[l - 1, i], lower, preferred_element_type=F32)
                image += jnp.dot(low[l - 1, i], upper, preferred_element_type=F32)
                change[s, x, y, l] += image[0:96]
                change[s, x, y, l - 1, 0:16] += image[96:112]
                change[s, x + 1, y, l, 64:80] += image[112:128]
                change[s, x, y + 1, l, 80:96] += image[128:144]

    def send_images(s, l):
        for k in (1, 2):
            m = 16 * (k - 1)
            out_ix[s, l - 1, m : m + 16] = change[s, 3, k, l, 64:80].astype(BF16)
            out_iy[s, l - 1, m : m + 16] = change[s, k, 3, l, 80:96].astype(BF16)
        send(s, IMAGE_X + l - 1, IMAGE_Y + l - 1)

    def send_images_z(s):
        for x in (1, 2):
            for y in (1, 2):
                m = 16 * (2 * x + y - 3)
                out_iz[s, m : m + 16] = change[s, x, y, 2, 0:16].astype(BF16)
        send(s, IMAGE_Z)

    def take_images(s, l):
        def from_x():
            for k in (0, 1):
                left[0, k, l, 64:80] -= in_ix[s, l - 1, 16 * k : 16 * k + 16].astype(F32)

        def from_y():
            for k in (0, 1):
                left[k, 0, l, 80:96] -= in_iy[s, l - 1, 16 * k : 16 * k + 16].astype(F32)

        receive(s, IMAGE_X + l - 1, from_x)
        receive(s, IMAGE_Y + l - 1, from_y)

    def take_images_z(s):
        def use():
            for x in (1, 2):
                for y in (1, 2):
                    m = 16 * (2 * x + y - 3)
                    change[s, x, y, 0, 0:16] += in_iz[s, m : m + 16].astype(F32)

        receive(s, IMAGE_Z, use)

    def update_own(s, l):
        rows = slice(0, 96) if l == 1 else slice(16, 96)
        for x in (1, 2):
            for y in (1, 2):
                left[x - 1, y - 1, l, rows] -= change[s, x, y, l, rows]
        clear_left()

    def update_late(s):
        for x in (1, 2):
            for y in (1, 2):
                left[x - 1, y - 1, 0, 0:16] -= change[s, x, y, 0, 0:16]
        clear_left()

    def write_early():
        for x in range(2):
            for y in range(2):
                for z in range(2):
                    block = total[0, x + 1, y + 1, z + 1] + total[1, x + 1, y + 1, z + 1]
                    solution_ref[x, y, 0:63, z, :] = block[16:79]
                    solution_ref[x, y, 63:72, z, :] = block[80:89]
                    lower = total[0, x + 1, y + 1, z, 0:16] + total[1, x + 1, y + 1, z, 0:16]
                    solution_ref[x, y, 72:81, z, :] = lower[0:9]
                    residual_ref[x, y, 0:63, z, :] = left[x, y, z + 1, 16:79]
                    residual_ref[x, y, 63:72, z, :] = left[x, y, z + 1, 80:89]
                residual_ref[x, y, 72:81, 1, :] = left[x, y, 1, 0:9]

    early = (EARLY_X, EARLY_Y, EARLY_XY)
    late = (LATE_X, LATE_Y, LATE_XY)
    back = (BACK_X, BACK_Y, BACK_XY)
    back2 = (BACK2_X, BACK2_Y, BACK2_XY)
    z_early = (Z_UPPER, Z_LOWER, Z_FACE)
    z_late = (Z_LAST_X, Z_LAST_Y)

    blank_total(0)
    for load in loads[1:]:
        load.wait()

    def separate(i, carry):
        x, y = i // 2, i % 2
        for k in range(5):
            width = min(128, PATCH - 128 * k)
            wide[k, :, 0:width] = pairs[x, y, :, 128 * k : 128 * k + width].astype(F32)
        for z in range(2):
            for k in range(5):
                width = min(128, PATCH - 128 * k)
                rows = wide[k, pl.ds(z, PATCH, stride=2), :].astype(BF16)
                held[x, y, z, :, 128 * k : 128 * k + width] = rows[:, 0:width]
        return carry

    lax.fori_loop(0, 4, separate, 0)
    send(0, *early)
    prepare(0, 0, 3)
    for s in range(SWEEPS):
        if s == 0:
            receive(s, Z_FIRST)
            send(s, LATE_X, LATE_XY)
            receive(s, Z_SECOND)
            send(s, LATE_Y)
            prepare(0, 3, 4)
            receive(s, Z_HALO)
            prepare(1, 0, 1)
            for number in early:
                receive(s, number)
        else:
            take_images_z(s - 1)
            update_late(s - 1)
            round_late(s)
            for number in z_early + z_late:
                receive(s, number)
            send(s, *late)
            for number in early:
                receive(s, number)
            solve(s, 1, False)
            solve(s, 1, True)
        for number in late:
            receive(s, number)
        solve(s, 0, False)
        send_back_z_first(s)
        send_back(s, (0,), back)
        solve(s, 0, True)
        if s == 0:
            prepare(1, 1, 3)
        else:
            send_back(s, (1, 2), back2)
        take_back(s, (0,), back)
        send_back_z(s)
        if s == 0:
            prepare(1, 3, 4)
            solve(s, 1, False)
            solve(s, 1, True)
            send_back(s, (1, 2), back2)
            lax.fori_loop(0, 4, elements, 0)
            blank_change(0)
        take_back(s, (1, 2), back2)
        if s < SWEEPS - 1:
            take_back_z(s)
            clear_total(s)
            images(s, 2)
            send_images(s, 2)
            update_own(s, 2)
            round_own(s + 1, 2)
            send(s + 1, *z_early)
            send_images_z(s)
            images(s, 1)
            send_images(s, 1)
            update_own(s, 1)
            take_images(s, 2)
            round_faces(s + 1)
            send(s + 1, *z_late)
            blank_total(s + 1)
            take_images(s, 1)
            round_own(s + 1, 1)
            send(s + 1, *early)
            blank_change(s + 1)
        else:
            clear_total(s)
            images(s, 1)
            send_images(s, 1)
            take_back_z(s)
            clear_total(s)
            images(s, 2)
            send_images_z(s)
            send_images(s, 2)
            update_own(s, 1)
            update_own(s, 2)
            write_early()
            take_images(s, 1)
            take_images(s, 2)

    for z in range(2):
        for k in range(2):
            residual_ref[0, k, 54:63, z, :] = left[0, k, z + 1, 70:79]
            residual_ref[k, 0, 63:72, z, :] = left[k, 0, z + 1, 80:89]
    take_images_z(SWEEPS - 1)
    update_late(SWEEPS - 1)
    for x in range(2):
        for y in range(2):
            residual_ref[x, y, 72:81, 0, :] = left[x, y, 0, 0:9]

    for copy, sends, _ in routes.values():
        if_(sends, copy.wait_send)


def body(residual_start, patch_inverse, patch_order, element_matrix, face_order):
    swapped = lambda value: jnp.transpose(value, (0, 1, 3, 2, 4))
    residual_start = swapped(residual_start)
    shape = jax.ShapeDtypeStruct(residual_start.shape, F32)
    vmem = pl.BlockSpec(memory_space=pltpu.VMEM)
    total, left = pl.pallas_call(
        kernel,
        out_shape=(shape, shape),
        in_specs=[pl.BlockSpec(memory_space=pltpu.HBM)] * 5,
        out_specs=(vmem, vmem),
        scratch_shapes=[
            pltpu.VMEM(residual_start.shape, F32),
            pltpu.VMEM(patch_order.shape, jnp.int32),
            pltpu.VMEM((2, 2, LOCAL, 2, LOCAL), F32),
            pltpu.VMEM((2, 2, 6, 2, FACE), jnp.int32),
            pltpu.VMEM((2, 2, 2 * PATCH, PATCH), BF16),
            pltpu.VMEM((5, 2 * PATCH, 128), F32),
            pltpu.VMEM((2, 2, 2, PATCH, PATCH), BF16),
            pltpu.VMEM((2, 4, STAR, STAR), BF16),
            pltpu.VMEM((2, 4, WIDE, WIDE), BF16),
            pltpu.VMEM((2, 4, WIDE, WIDE), BF16),
            pltpu.VMEM((SWEEPS, 3, 3, 3, BLOCK, 128), BF16),
            pltpu.VMEM((SWEEPS, 4, 4, 3, BLOCK, 128), F32),
            pltpu.VMEM((SWEEPS, 4, 4, 3, BLOCK, 128), F32),
            pltpu.VMEM((2, 2, 3, BLOCK, 128), F32),
            pltpu.VMEM((SWEEPS, 3, 2, 112, 128), BF16),
            pltpu.VMEM((SWEEPS, 3, 2, 112, 128), BF16),
            pltpu.VMEM((SWEEPS, 3, 128, 128), BF16),
            pltpu.VMEM((SWEEPS, 3, 2, 112, 128), BF16),
            pltpu.VMEM((SWEEPS, 3, 2, 112, 128), BF16),
            pltpu.VMEM((SWEEPS, 3, 128, 128), BF16),
            pltpu.VMEM((SWEEPS, 448, 128), BF16),
            pltpu.VMEM((SWEEPS, 448, 128), BF16),
            pltpu.VMEM((SWEEPS, 2, 32, 128), BF16),
            pltpu.VMEM((SWEEPS, 2, 32, 128), BF16),
            pltpu.VMEM((SWEEPS, 64, 128), BF16),
            pltpu.VMEM((SWEEPS, 2, 32, 128), BF16),
            pltpu.VMEM((SWEEPS, 2, 32, 128), BF16),
            pltpu.VMEM((SWEEPS, 64, 128), BF16),
            pltpu.SemaphoreType.DMA((8,)),
            pltpu.SemaphoreType.DMA((SWEEPS, COPIES)),
            pltpu.SemaphoreType.DMA((SWEEPS, COPIES)),
        ],
        compiler_params=pltpu.CompilerParams(
            collective_id=0, has_side_effects=True, vmem_limit_bytes=60 * 1024 * 1024
        ),
    )(residual_start, swapped(patch_inverse), patch_order, swapped(element_matrix), swapped(face_order))

    def finish(first, second, first_out, second_out, sem):
        copies = [
            pltpu.make_async_copy(first, first_out, sem.at[0]),
            pltpu.make_async_copy(second, second_out, sem.at[1]),
        ]
        for copy in copies:
            copy.start()
        for copy in copies:
            copy.wait()

    total, left = pl.pallas_call(
        finish,
        out_shape=(shape, shape),
        in_specs=[vmem, vmem],
        out_specs=(pl.BlockSpec(memory_space=pltpu.HBM), pl.BlockSpec(memory_space=pltpu.HBM)),
        scratch_shapes=[pltpu.SemaphoreType.DMA((2,))],
    )(total, left)
    return swapped(total), swapped(left)


def solution(mesh):
    return jax.shard_map(
        body,
        mesh=mesh,
        in_specs=(
            P("gx", "gy", "gz", None, None),
            P("gx", "gy", "gz", None, None),
            P("gx", "gy", "gz", None),
            P("gx", "gy", "gz", None, None),
            P("gx", "gy", "gz", None, None),
        ),
        out_specs=(P("gx", "gy", "gz", None, None), P("gx", "gy", "gz", None, None)),
        check_vma=False,
    )
```
